32 devices in a mesh: dom: 8 (over z, y), dir: 4 (over x, core).
Axes of the slice: x: 2, y: 2, z: 4, core: 2. Of those that a mesh axis runs over, the one named last changes fastest.
Arguments:
- unknowns: bfloat16 [128, 8, 1024], P(('dom', 'dir')), may hold values from -6 to 6
- schur_blocks: bfloat16 [128, 1024, 1024], P(('dom', 'dir')), may hold values from -0.1875 to 0.1875
- adjacency: int32 [128, 4], P(('dom', 'dir')), may hold values from 0 to 127, as said below
- row_map: int32 [128, 4, 1024], P(('dom', 'dir')), may hold values from 0 to 1023
- coupling: float32 [128, 4, 1024], P(('dom', 'dir')), may hold values from -1.5 to 1.5
- owner_box: int32 [128, 256, 1], P(('dom', 'dir')), may hold values from 0 to 255; in each aligned block of 1024 rows (0 to 1023, 1024 to 2047, ..., all dimensions but the last counted through in order) at most 8 rows name the same one
- aggregation: bfloat16 [256, 256, 1152], P('dom', None, 'dir'), may hold values from -0.1875 to 0.1875
- trans_table: float32 [316, 1152], P(None, 'dir'), may hold values from -1.5 to 1.5
- inter_list: int32 [256, 16], P('dom'), may hold values from 0 to 255, as said below
- inter_type: int32 [256, 16], P('dom'), may hold values from 0 to 315
- near_list: int32 [256, 4], P(('dom', 'dir')), may hold values from 0 to 31
- near_blocks: bfloat16 [256, 4, 256, 256], P(('dom', 'dir')), may hold values from -0.375 to 0.375
Outputs:
- response: float32 [128, 8, 1024], P(('dom', 'dir'))
The draws below stay inside these ranges and needn't reach their ends.
Inputs may be any that keep to these rules, and one draw needn't show every extreme that they name: `adjacency`: every neighbour t of subdomain s has t // 16 equal to g - 1, g or g + 1 modulo 8, with g = s // 16, and (t // 4) % 4 = (s // 4) % 4. `owner_box`: among the surface unknowns of one aligned block of 4 subdomains, no box is named more than 8 times. `inter_list`: every source box c of box b has c // 32 equal to b // 32 - 1, b // 32 or b // 32 + 1 modulo 8.
All inputs are finite; a program needn't handle non-finite values.
Results may differ from the reference program's by a relative error of at most 0.0035.
Values may be sent and summed in bfloat16 or wider, within the bound.
A program may use at most 128 MiB of HBM per device.

```python
import math
import jax
import jax.numpy as jnp
import numpy as np
from jax import lax

SUB_DEV = 4
ROWS_SUB = 1024
SURF_ROWS = 256
EXCITES = 8
ADJ_COUNT = 4
BOX_SLOTS = 256
DIRECTIONS = 1152
LIST_LEN = 16
TRANS_TYPES = 316
NEAR_BLOCKS = 4
BOX_DEV = 8
SUBDOMAINS = 128
BOXES = 256
BOX_GRP = 32
SLOT_CAP = 8
N_DOM = 8
N_DIR = 4


def draw_adjacency(key, part):
    subdomains = SUB_DEV * N_DOM * N_DIR
    first_key, second_key = jax.random.split(jax.random.fold_in(key, 11))
    shifted = jax.random.randint(first_key, (subdomains, ADJ_COUNT), -1, 2)
    within = jax.random.randint(second_key, (subdomains, ADJ_COUNT), 0, SUB_DEV)
    device = jnp.arange(subdomains, dtype=jnp.int32)[:, None] // SUB_DEV
    dom_of = device // N_DIR
    dir_of = device % N_DIR
    target = (dom_of + shifted + N_DOM) % N_DOM * N_DIR + dir_of
    return (target * SUB_DEV + within).astype(jnp.int32)


def draw_inter_list(key, part):
    group_boxes = BOX_DEV * N_DIR
    box_total = group_boxes * N_DOM
    first_key, second_key = jax.random.split(jax.random.fold_in(key, 23))
    shifted = jax.random.randint(first_key, (box_total, LIST_LEN), -1, 2)
    within = jax.random.randint(second_key, (box_total, LIST_LEN), 0, group_boxes)
    group_of = jnp.arange(box_total, dtype=jnp.int32)[:, None] // group_boxes
    target = (group_of + shifted + N_DOM) % N_DOM
    return (target * group_boxes + within).astype(jnp.int32)


def with_ends(result, rng, low, largest):
    longest = result.shape.index(max(result.shape))
    spots = []
    for shift in (0, 1):
        where = [jax.random.randint(jax.random.fold_in(rng, axis), (), 0, length) for axis, length in enumerate(result.shape)]
        where[longest] = (where[longest] + shift) % result.shape[longest]
        spots.append(tuple(where))
    return result.at[spots[0]].set(low).at[spots[1]].set(largest)


def block_levels(own_key, extent, cuts, smallest, top_value):
    gain, own = 1.0, jax.random.fold_in(own_key, 6)
    for position, shards_of in cuts:
        steps = jnp.exp(jax.random.uniform(jax.random.fold_in(own, position), (shards_of,), jnp.float32, smallest / len(cuts), top_value / len(cuts)))
        gain = gain * jnp.repeat(steps, extent[position] // shards_of).reshape([-1 if axis == position else 1 for axis in range(len(extent))])
    return gain


def deal_out(own_key, own, number, rows, number_of, top, limit, slope):
    sequence = jax.random.permutation(own_key, number_of)
    packed, ordinary = portions_of(number_of, rows * top, limit, slope, True), portions_of(number_of, rows * top, limit, slope, False)
    places = jnp.arange(number_of)

    def named(lengths, offset_by):
        used = int((lengths > 0).sum())
        fixed = max(1, used // 4)
        moved = fixed + (places - fixed + offset_by * (used - fixed)) % max(1, number_of - fixed)
        return jnp.zeros((number_of,), jnp.int32).at[sequence[jnp.where(places < fixed, places, moved)]].set(jnp.asarray(lengths, jnp.int32))

    lengths = jnp.where(number % 4 == 0, named(packed, number // 4), named(ordinary, number - number // 4 - 1))
    mixed = jax.random.permutation(jax.random.fold_in(own, 3), number_of)
    source_of, sink = mixed[0:number_of // 2 * 2:2], mixed[1:number_of // 2 * 2:2]
    room = jnp.minimum(lengths[source_of] - 1, limit - lengths[sink]) // 2
    room = jnp.where((source_of == sequence[0]) | (sink == sequence[0]) | (lengths[sink] == 0), 0, jnp.maximum(room, 0))
    moved = jax.random.randint(jax.random.fold_in(own, 4), (number_of // 2,), 0, 1 << 20) % (room + 1)
    lengths = lengths.at[source_of].add(-moved).at[sink].add(moved)
    labels = jnp.searchsorted(jnp.cumsum(lengths), jnp.arange(rows * top), side="right").astype(jnp.int32)
    table = labels.reshape(top, rows).T
    table = table[jax.random.permutation(jax.random.fold_in(own, 1), rows)]
    offset_by = jax.random.randint(jax.random.fold_in(own, 2), (rows, 1), 0, top)
    return jnp.take_along_axis(table, (jnp.arange(top)[None, :] + offset_by) % top, axis=1)


def portions_of(count, total, limit, skew, full):
    loads = [(1 << 20) // math.isqrt(standing ** skew) + 1 for standing in range(1, count + 1)]
    largest = limit if full else min(limit, max(-(-total // count), total * loads[0] // sum(loads)))
    least = 1 if total - largest >= count - 1 else 0
    holding, rest = [largest] + [least] * (count - 1), total - largest - least * (count - 1)
    while rest > 0:
        free = [i for i in range(1, count) if holding[i] < largest] or [i for i in range(1, count) if holding[i] < limit]
        mass, remaining = sum([loads[i] for i in free]), rest
        for i in free:
            more = min(limit - holding[i], max(1, remaining * loads[i] // mass), rest)
            holding[i] = holding[i] + more
            rest = rest - more
    return np.array(holding)


def gaussian(rng, dims, deviation, reach, pieces=(), held_as=jnp.bfloat16):
    result = jax.random.normal(rng, dims, jnp.float32) * deviation
    if len(pieces) > 0:
        result = block_levels(rng, dims, pieces, -0.22, 0.18) * result
    return jnp.clip(result, min=-reach, max=reach).astype(held_as)


def setup_inputs(seed: int = 0) -> dict:
    seeds = jax.random.split(jax.random.key(seed), 13)
    unknowns = gaussian(seeds[0], (SUBDOMAINS, EXCITES, ROWS_SUB), 1.0, 6.0, ((0, 32),))
    schur_blocks = gaussian(seeds[1], (SUBDOMAINS, ROWS_SUB, ROWS_SUB), ROWS_SUB ** -0.5, 0.1875, ((0, 32),))
    adjacency = draw_adjacency(jax.random.fold_in(seeds[12], 71), 0)
    row_map = with_ends(jax.random.randint(seeds[3], (SUBDOMAINS, ADJ_COUNT, ROWS_SUB), 0, ROWS_SUB), jax.random.fold_in(seeds[3], 1), 0, ROWS_SUB - 1).astype(jnp.int32)
    coupling = gaussian(seeds[4], (SUBDOMAINS, ADJ_COUNT, ROWS_SUB), 0.3, 1.5, ((0, 32),), jnp.float32)
    owner_box_keys = jax.random.split(jax.random.fold_in(seeds[5], 1), SUBDOMAINS * SURF_ROWS // (SUB_DEV * SURF_ROWS))
    owner_box_turns = jax.random.permutation(jax.random.fold_in(seeds[5], 3), SUBDOMAINS * SURF_ROWS // (SUB_DEV * SURF_ROWS))
    owner_box = jax.vmap(lambda own, number: deal_out(jax.random.fold_in(seeds[5], 2), own, number, SUB_DEV * SURF_ROWS, BOXES, 1, SLOT_CAP, 2))(owner_box_keys, owner_box_turns).reshape((SUBDOMAINS, SURF_ROWS, 1))
    aggregation = gaussian(seeds[6], (BOXES, BOX_SLOTS, DIRECTIONS), DIRECTIONS ** -0.5, 0.1875, ((0, 8), (2, 4)))
    trans_table = gaussian(seeds[7], (TRANS_TYPES, DIRECTIONS), 0.25, 1.5, ((1, 4),), jnp.float32)
    inter_list = draw_inter_list(jax.random.fold_in(seeds[12], 71), 0)
    inter_type = with_ends(jax.random.randint(seeds[9], (BOXES, LIST_LEN), 0, TRANS_TYPES), jax.random.fold_in(seeds[9], 1), 0, TRANS_TYPES - 1).astype(jnp.int32)
    near_list = with_ends(jax.random.randint(seeds[10], (BOXES, NEAR_BLOCKS), 0, BOX_GRP), jax.random.fold_in(seeds[10], 1), 0, BOX_GRP - 1).astype(jnp.int32)
    near_blocks = gaussian(seeds[11], (BOXES, NEAR_BLOCKS, BOX_SLOTS, BOX_SLOTS), BOX_SLOTS ** -0.5, 0.375, ((0, 32),))
    return dict(unknowns=unknowns, schur_blocks=schur_blocks, adjacency=adjacency, row_map=row_map, coupling=coupling, owner_box=owner_box, aggregation=aggregation, trans_table=trans_table, inter_list=inter_list, inter_type=inter_type, near_list=near_list, near_blocks=near_blocks)


def slot_ranks(owners):
    amount = owners.shape[0]
    same = owners[:, None] == owners[None, :]
    order = jnp.arange(amount, dtype=jnp.int32)
    earlier = order[:, None] > order[None, :]
    return jnp.sum(jnp.where(same & earlier, 1, 0), axis=1).astype(jnp.int32)


def reference(unknowns, schur_blocks, adjacency, row_map, coupling, owner_box, aggregation, trans_table, inter_list, inter_type, near_list, near_blocks):
    devices = N_DOM * N_DIR
    group_boxes = BOX_DEV * N_DIR
    box_total = group_boxes * N_DOM
    capacity = BOX_SLOTS // devices
    subdomains = SUB_DEV * devices
    dir_block = DIRECTIONS // N_DIR

    def schur_one(operands):
        return jnp.dot(operands[1], operands[0].T, preferred_element_type=jnp.float32)

    schur_part = lax.map(schur_one, (schur_blocks, unknowns))

    picked = unknowns[adjacency]
    row_index = jnp.broadcast_to(row_map[:, :, None, :], picked.shape)
    fetched = jnp.take_along_axis(picked, row_index, axis=3).astype(jnp.float32)
    coupled = jnp.sum(coupling[:, :, None, :] * fetched, axis=1)

    owners = owner_box[:, :, 0].reshape(devices, SUB_DEV * SURF_ROWS)
    slot_rank = lax.map(slot_ranks, owners)
    device = jnp.arange(devices, dtype=jnp.int32)[:, None]
    slot_index = ((device % N_DIR) * N_DOM + device // N_DIR) * capacity + slot_rank
    flat_index = (owners * BOX_SLOTS + slot_index).reshape(-1).astype(jnp.int32)
    surface = jnp.transpose(unknowns[:, :, :SURF_ROWS], (0, 2, 1)).reshape(-1, EXCITES)
    currents = jnp.zeros((box_total * BOX_SLOTS, EXCITES), jnp.bfloat16).at[flat_index].set(surface)
    currents = jnp.transpose(currents.reshape(box_total, BOX_SLOTS, EXCITES), (0, 2, 1))

    agg_groups = aggregation.reshape(N_DOM, group_boxes, BOX_SLOTS, DIRECTIONS)
    current_groups = currents.reshape(N_DOM, group_boxes, EXCITES, BOX_SLOTS)

    def radiate(operands):
        return jnp.einsum("hpd,hep->hed", operands[0].astype(jnp.float32), operands[1].astype(jnp.float32)).astype(jnp.bfloat16)

    patterns = lax.map(radiate, (agg_groups, current_groups)).reshape(box_total, EXCITES, DIRECTIONS)

    def respond(operands):
        listed, kinds, agg_part, nearest, blocks, group_current = operands
        sources = patterns[listed].astype(jnp.float32)
        factors = trans_table[kinds]
        incoming = jnp.einsum("hjd,hjed->hed", factors, sources).astype(jnp.bfloat16)
        agg_blocks = agg_part.astype(jnp.float32).reshape(group_boxes, BOX_SLOTS, N_DIR, dir_block)
        in_blocks = incoming.astype(jnp.float32).reshape(group_boxes, EXCITES, N_DIR, dir_block)
        far_terms = jnp.einsum("hpkd,hekd->khep", agg_blocks, in_blocks).astype(jnp.bfloat16)
        far_terms = lax.optimization_barrier(far_terms)
        far_part = jnp.sum(far_terms.astype(jnp.float32), axis=0)
        near_current = group_current[nearest].astype(jnp.float32)
        near_part = jnp.einsum("hjpq,hjeq->hep", blocks.astype(jnp.float32), near_current)
        return (far_part + near_part).astype(jnp.bfloat16)

    box_fields = lax.map(respond, (
        inter_list.reshape(N_DOM, group_boxes, LIST_LEN),
        inter_type.reshape(N_DOM, group_boxes, LIST_LEN),
        agg_groups,
        near_list.reshape(N_DOM, group_boxes, NEAR_BLOCKS),
        near_blocks.reshape(N_DOM, group_boxes, NEAR_BLOCKS, BOX_SLOTS, BOX_SLOTS),
        current_groups,
    )).reshape(box_total, EXCITES, BOX_SLOTS)

    field_table = jnp.transpose(box_fields, (0, 2, 1)).reshape(box_total * BOX_SLOTS, EXCITES)
    surface_field = field_table[flat_index].reshape(subdomains, SURF_ROWS, EXCITES)
    surface_field = jnp.transpose(surface_field, (0, 2, 1)).astype(jnp.float32)
    combined = schur_part + coupled
    return combined.at[:, :, :SURF_ROWS].add(surface_field)
```

```python
import functools

import jax
import jax.numpy as jnp
from jax import lax
from jax.experimental import pallas as pl
from jax.experimental.pallas import tpu as pltpu
from jax.sharding import PartitionSpec as P

MESH = pl.DeviceIdType.MESH
LANES = 128
F32 = jnp.float32
BF16 = jnp.bfloat16


def dot(a, b, ca, cb):
    return lax.dot_general(a, b, (((ca,), (cb,)), ((), ())), preferred_element_type=F32)


def iota(shape, dim):
    return lax.broadcasted_iota(jnp.int32, shape, dim)


def shift_of(value):
    bits = value.bit_length() - 1
    assert value == 1 << bits
    return bits


def kernel(
    dims,
    adj_ref,
    list_ref,
    type_ref,
    near_ref,
    unk_ref,
    owner_ref,
    agg_hbm,
    trans_hbm,
    maps_hbm,
    coup_hbm,
    schur_hbm,
    blocks_hbm,
    out_ref,
    agg_v,
    trans_v,
    trans_t,
    maps_v,
    coup_v,
    schur_v,
    blocks_v,
    place,
    perm,
    send1,
    recv1,
    recv0,
    winf,
    curf,
    pats,
    recv2,
    patf,
    coupled,
    nearf,
    total,
    send3,
    recv3,
    local_sem,
    schur_sem,
    send_sem,
    recv_sem,
    side_send,
    side_recv,
    wide_send,
    wide_recv,
):
    doms, dirs = dims
    devices = doms * dirs
    subs, excites, rows = unk_ref.shape
    boxes, directions, slots = agg_v.shape
    near_count, own = near_ref.shape
    adj_count = adj_ref.shape[1]
    list_len = list_ref.shape[0]
    surface = owner_ref.shape[1] // subs
    capacity = slots // devices
    per_tile = LANES // excites
    halves = boxes // per_tile
    unit = max(16, halves * capacity)
    amount = subs * surface
    all_rows = devices * unit
    my_dom = lax.axis_index("dom")
    my_dir = lax.axis_index("dir")
    me = my_dom * dirs + my_dir
    my_slot = my_dir * doms + my_dom
    right, left = lax.rem(my_dom + 1, doms), lax.rem(my_dom + doms - 1, doms)

    barrier = pltpu.get_barrier_semaphore()

    def greet(k, carry):
        other = lax.rem(me + k, devices)
        pl.semaphore_signal(
            barrier,
            inc=1,
            device_id=(lax.div(other, dirs), lax.rem(other, dirs)),
            device_id_type=MESH,
        )
        return carry

    lax.fori_loop(1, devices, greet, 0)

    locals_ = [
        pltpu.make_async_copy(src, dst, local_sem.at[i])
        for i, (src, dst) in enumerate(
            [
                (agg_hbm, agg_v),
                (trans_hbm, trans_t),
                (maps_hbm, maps_v),
                (coup_hbm, coup_v),
                (blocks_hbm, blocks_v),
            ]
        )
    ]
    schurs = [
        pltpu.make_async_copy(schur_hbm.at[s], schur_v.at[s], schur_sem.at[s]) for s in range(subs)
    ]
    locals_[0].start()
    schurs[0].start()
    schurs[1].start()
    locals_[4].start()
    for i in (1, 2, 3):
        locals_[i].start()
    for s in range(2, subs):
        schurs[s].start()

    owner_row = owner_ref[...]
    owner_col = jnp.concatenate(
        [
            jnp.broadcast_to(owner_row[:, k : k + LANES], (LANES, LANES)).T
            for k in range(0, amount, LANES)
        ],
        axis=0,
    )
    order = iota((amount, LANES), 0)
    ahead = order - iota((amount, LANES), 1)
    ranks = []
    for k in range(0, amount, LANES):
        same = (owner_col == owner_row[:, k : k + LANES]) & (ahead < k)
        ranks.append(jnp.sum(jnp.where(same, 1.0, 0.0), axis=0, keepdims=True))
    rank = jnp.concatenate(ranks, axis=1).astype(jnp.int32)
    half = (owner_row & (boxes - 1)) >> shift_of(per_tile)
    key = (owner_row >> shift_of(boxes)) * unit + half * capacity + rank
    place[...] = jnp.where(iota((doms * unit, amount), 0) == key, 1.0, 0.0).astype(BF16)
    wide = []
    for s in range(subs):
        piece = unk_ref[s][:, :surface].astype(F32)
        wide.append(jnp.concatenate([piece] * per_tile, axis=0).T)
    wide = jnp.concatenate(wide, axis=0)
    lane_box = iota((amount, LANES), 1) >> shift_of(excites)
    wide = jnp.where((owner_col & (per_tile - 1)) == lane_box, wide, 0.0).astype(BF16)
    send1[...] = dot(place[...], wide, 1, 0).astype(BF16)

    row = iota((all_rows, slots), 0)
    col = iota((all_rows, slots), 1)
    within = row & (unit - 1)
    slot_of = (row >> shift_of(unit)) * capacity + (within & (capacity - 1))
    for h in range(halves):
        hit = (slot_of == col) & ((within >> shift_of(capacity)) == h)
        perm[h] = jnp.where(hit, 1.0, 0.0).astype(BF16)

    pl.semaphore_wait(barrier, devices - 1)

    def tile(index):
        return pl.ds(pl.multiple_of(index * unit, unit), unit)

    def scatter(k, carry):
        other = lax.rem(me + k, devices)
        to_dom, to_dir = lax.div(other, dirs), lax.rem(other, dirs)
        pltpu.make_async_remote_copy(
            src_ref=send1.at[tile(to_dom)],
            dst_ref=recv1.at[tile(my_slot)],
            send_sem=send_sem.at[0],
            recv_sem=recv_sem.at[0],
            device_id=(to_dom, to_dir),
            device_id_type=MESH,
        ).start()
        return carry

    lax.fori_loop(1, devices, scatter, 0)
    recv1[tile(my_slot), :] = send1[tile(my_dom), :]

    sides = []
    for side, target in enumerate((right, left)):
        copy = pltpu.make_async_remote_copy(
            src_ref=unk_ref,
            dst_ref=recv0.at[side],
            send_sem=side_send.at[side],
            recv_sem=side_recv.at[side],
            device_id=(target, my_dir),
            device_id_type=MESH,
        )
        copy.start()
        sides.append(copy)

    block = 256

    def schur(s):
        schurs[s].wait()
        unknown = unk_ref[s]

        def part(i, carry):
            at = pl.ds(pl.multiple_of(i * block, block), block)
            out_ref[s, :, at] = dot(unknown, schur_v[s, at, :], 1, 1)
            return carry

        lax.fori_loop(0, rows // block, part, 0)

    schur(0)
    schur(1)

    def drain(buffer, sem):
        size = pl.ds(0, all_rows - unit)
        pltpu.make_async_copy(buffer.at[size], buffer.at[size], sem).wait()

    drain(recv1, recv_sem.at[0])
    arrived = recv1[...]
    for h in range(halves):
        piece = dot(arrived, perm[h], 0, 0)
        curf[h * per_tile : (h + 1) * per_tile] = piece.reshape(per_tile, excites, slots)

    locals_[0].wait()
    chunks = 4
    chunk_boxes = boxes // chunks
    pair = 2
    wides = []
    for c in range(chunks):

        def radiate(i, carry):
            first = c * chunk_boxes + i * pair
            found = []
            for k in range(pair):
                b = first + k
                found.append(dot(curf[b].astype(BF16), agg_v[b], 1, 1))
            both = jnp.concatenate(found, axis=0).astype(BF16)
            pats[pl.ds(pl.multiple_of(first * excites, 16), 16), :] = both
            patf[pl.ds(boxes + first, pair)] = both.astype(F32).reshape(pair, excites, directions)
            return carry

        lax.fori_loop(0, chunk_boxes // pair, radiate, 0)
        at = pl.ds(c * chunk_boxes * excites, chunk_boxes * excites)
        for side, target in enumerate((right, left)):
            copy = pltpu.make_async_remote_copy(
                src_ref=pats.at[at],
                dst_ref=recv2.at[side, at],
                send_sem=wide_send.at[side, c],
                recv_sem=wide_recv.at[side, c],
                device_id=(target, my_dir),
                device_id_type=MESH,
            )
            copy.start()
            wides.append(copy)

    locals_[1].wait()
    trans_v[...] = trans_t[...].T

    locals_[4].wait()
    nearf[...] = jnp.zeros_like(nearf)

    def near(b, carry):
        field = jnp.zeros((excites, slots), F32)
        for j in range(near_count):
            source = curf[near_ref[j, b]].astype(BF16)
            field = field + dot(source, blocks_v[b, j], 1, 1)
        nearf[my_dir * own + b] = field
        return carry

    lax.fori_loop(0, own, near, 0)

    for copy in sides:
        copy.wait_recv()
    winf[0:subs] = recv0[0].astype(F32)
    winf[subs : 2 * subs] = unk_ref[...].astype(F32)
    winf[2 * subs : 3 * subs] = recv0[1].astype(F32)
    locals_[2].wait()
    locals_[3].wait()
    group_subs = subs * dirs
    sub_base = left * group_subs

    def couple(s, carry):
        fields = [jnp.zeros((excites, LANES), F32)] * (rows // LANES)
        for k in range(adj_count):
            offset = adj_ref[s, k] - sub_base
            offset = jnp.where(offset < 0, offset + group_subs * doms, offset)
            offset = jnp.minimum(offset, 3 * group_subs - 1)
            source = winf[lax.div(offset, group_subs) * subs + lax.rem(offset, subs)]
            mapping = maps_v[s, k : k + 1, :]
            factor = coup_v[s, k : k + 1, :]
            for c in range(rows // LANES):
                at = slice(c * LANES, (c + 1) * LANES)
                index = jnp.broadcast_to(mapping[:, at], (excites, LANES))
                low, high = index & (LANES - 1), index >> shift_of(LANES)
                value = jnp.zeros((excites, LANES), F32)
                for q in range(rows // LANES):
                    got = jnp.take_along_axis(
                        source[:, q * LANES : (q + 1) * LANES],
                        low,
                        axis=1,
                        mode="promise_in_bounds",
                    )
                    value = jnp.where(high == q, got, value)
                fields[c] = fields[c] + factor[:, at] * value
        coupled[s] = jnp.concatenate(fields, axis=1)
        return carry

    lax.fori_loop(0, subs, couple, 0)
    for s in range(2, subs - 1):
        schur(s)

    for copy in wides:
        copy.wait_recv()
    for side, base in ((0, 0), (1, 2 * boxes)):
        patf[base : base + boxes] = recv2[side].astype(F32).reshape(boxes, excites, directions)

    box_base = left * boxes

    def respond(i, carry):
        first = i * pair
        found = []
        for k in range(pair):
            b = first + k
            field = jnp.zeros((excites, directions), F32)
            for j in range(list_len):
                offset = list_ref[j, b] - box_base
                offset = jnp.where(offset < 0, offset + boxes * doms, offset)
                offset = jnp.minimum(offset, 3 * boxes - 1)
                field = field + trans_v[pl.ds(type_ref[j, b], 1), :] * patf[offset]
            found.append(dot(field.astype(BF16), agg_v[b], 1, 0) + nearf[b])
        both = jnp.concatenate(found, axis=0).astype(BF16)
        total[pl.ds(pl.multiple_of(first * excites, 16), 16), :] = both
        return carry

    lax.fori_loop(0, boxes // pair, respond, 0)
    leaving = jnp.zeros((all_rows, LANES), F32)
    for h in range(halves):
        leaving = leaving + dot(perm[h], total[h * LANES : (h + 1) * LANES, :], 1, 1)
    send3[...] = leaving.astype(BF16)

    def give_back(k, carry):
        other = lax.rem(me + k, devices)
        to_dom, to_dir = lax.div(other, dirs), lax.rem(other, dirs)
        pltpu.make_async_remote_copy(
            src_ref=send3.at[tile(to_dir * doms + to_dom)],
            dst_ref=recv3.at[tile(my_slot)],
            send_sem=send_sem.at[1],
            recv_sem=recv_sem.at[1],
            device_id=(to_dom, to_dir),
            device_id_type=MESH,
        ).start()
        return carry

    lax.fori_loop(1, devices, give_back, 0)
    recv3[tile(my_slot), :] = send3[tile(my_slot), :]

    schur(subs - 1)

    drain(recv3, recv_sem.at[1])
    group_rows = doms * unit
    field = jnp.zeros((group_rows, LANES), F32)
    for r in range(dirs):
        field = field + recv3[r * group_rows : (r + 1) * group_rows, :].astype(F32)
    back = dot(field.T.astype(BF16), place[...], 1, 0)
    sub_box = iota((LANES, amount), 0) >> shift_of(excites)
    back = jnp.where((owner_row & (per_tile - 1)) == sub_box, back, 0.0)
    back = jnp.sum(back.reshape(per_tile, excites, amount), axis=0)
    for s in range(subs):
        add = coupled[s]
        out_ref[s, :, :surface] += add[:, :surface] + back[:, s * surface : (s + 1) * surface]
        out_ref[s, :, surface:] += add[:, surface:]

    for copy in sides:
        copy.wait_send()
    for copy in wides:
        copy.wait_send()
    drain(recv1, send_sem.at[0])
    drain(recv3, send_sem.at[1])


def shards(
    mesh_dims,
    unknowns,
    schur_blocks,
    adjacency,
    row_map,
    coupling,
    owner_box,
    aggregation,
    trans_table,
    inter_list,
    inter_type,
    near_list,
    near_blocks,
):
    doms, dirs = mesh_dims
    subs, excites, rows = unknowns.shape
    boxes, slots, directions = aggregation.shape
    capacity = slots // (doms * dirs)
    per_tile = LANES // excites
    halves = boxes // per_tile
    unit = max(16, halves * capacity)
    all_rows = doms * dirs * unit
    amount = subs * owner_box.shape[1]
    vmem = pl.BlockSpec(memory_space=pltpu.VMEM)
    smem = pl.BlockSpec(memory_space=pltpu.SMEM)
    hbm = pl.BlockSpec(memory_space=pl.ANY)
    dma = pltpu.SemaphoreType.DMA
    scratch = [
        pltpu.VMEM((boxes, directions, slots), BF16),
        pltpu.VMEM(trans_table.shape, F32),
        pltpu.VMEM(trans_table.shape[::-1], F32),
        pltpu.VMEM(row_map.shape, jnp.int32),
        pltpu.VMEM(coupling.shape, F32),
        pltpu.VMEM(schur_blocks.shape, BF16),
        pltpu.VMEM(near_blocks.shape, BF16),
        pltpu.VMEM((doms * unit, amount), BF16),
        pltpu.VMEM((halves, all_rows, slots), BF16),
        pltpu.VMEM((doms * unit, LANES), BF16),
        pltpu.VMEM((all_rows, LANES), BF16),
        pltpu.VMEM((2, subs, excites, rows), BF16),
        pltpu.VMEM((3 * subs, excites, rows), F32),
        pltpu.VMEM((boxes, excites, slots), F32),
        pltpu.VMEM((boxes * excites, directions), BF16),
        pltpu.VMEM((2, boxes * excites, directions), BF16),
        pltpu.VMEM((3 * boxes, excites, directions), F32),
        pltpu.VMEM((subs, excites, rows), F32),
        pltpu.VMEM((boxes, excites, slots), F32),
        pltpu.VMEM((boxes * excites, slots), BF16),
        pltpu.VMEM((all_rows, LANES), BF16),
        pltpu.VMEM((all_rows, LANES), BF16),
        dma((5,)),
        dma((subs,)),
        dma((2,)),
        dma((2,)),
        dma((2,)),
        dma((2,)),
        dma((2, 4)),
        dma((2, 4)),
    ]
    return pl.pallas_call(
        functools.partial(kernel, mesh_dims),
        out_shape=jax.ShapeDtypeStruct(unknowns.shape, F32),
        in_specs=[smem] * 4 + [vmem] * 2 + [hbm] * 6,
        out_specs=vmem,
        scratch_shapes=scratch,
        compiler_params=pltpu.CompilerParams(
            collective_id=0, has_side_effects=True, vmem_limit_bytes=56 * 1024 * 1024
        ),
    )(
        adjacency,
        inter_list.T,
        inter_type.T,
        near_list.T,
        unknowns,
        owner_box.reshape(1, amount),
        jnp.swapaxes(aggregation, 1, 2),
        trans_table.T,
        row_map,
        coupling,
        schur_blocks,
        near_blocks,
    )


def solution(mesh):
    in_specs = (
        P(("dom", "dir"), None, None),
        P(("dom", "dir"), None, None),
        P(("dom", "dir"), None),
        P(("dom", "dir"), None, None),
        P(("dom", "dir"), None, None),
        P(("dom", "dir"), None, None),
        P("dom", None, "dir"),
        P(None, "dir"),
        P("dom", None),
        P("dom", None),
        P(("dom", "dir"), None),
        P(("dom", "dir"), None, None, None),
    )
    out_specs = P(("dom", "dir"), None, None)
    dims = (mesh.shape["dom"], mesh.shape["dir"])
    return jax.shard_map(
        functools.partial(shards, dims),
        mesh=mesh,
        in_specs=in_specs,
        out_specs=out_specs,
        check_vma=False,
    )
```

```python
import functools

import jax
import jax.numpy as jnp
from jax import lax
from jax.experimental import pallas as pl
from jax.experimental.pallas import tpu as pltpu
from jax.sharding import PartitionSpec as P

MESH = pl.DeviceIdType.MESH
LANES = 128
F32 = jnp.float32
BF16 = jnp.bfloat16


def dot(a, b, ca, cb):
    return lax.dot_general(a, b, (((ca,), (cb,)), ((), ())), preferred_element_type=F32)


def iota(shape, dim):
    return lax.broadcasted_iota(jnp.int32, shape, dim)


def shift_of(value):
    bits = value.bit_length() - 1
    assert value == 1 << bits
    return bits


def kernel(
    dims,
    adj_ref,
    list_ref,
    type_ref,
    near_ref,
    unk_ref,
    owner_ref,
    agg_hbm,
    trans_hbm,
    maps_hbm,
    coup_hbm,
    schur_hbm,
    blocks_hbm,
    out_ref,
    agg_v,
    trans_v,
    trans_t,
    maps_v,
    coup_v,
    schur_v,
    blocks_v,
    place,
    perm,
    send1,
    recv1,
    recv0,
    winf,
    curf,
    pats,
    recv2,
    patf,
    coupled,
    nearf,
    total,
    send3,
    recv3,
    local_sem,
    schur_sem,
    send_sem,
    recv_sem,
    side_send,
    side_recv,
    wide_send,
    wide_recv,
):
    doms, dirs = dims
    devices = doms * dirs
    subs, excites, rows = unk_ref.shape
    boxes, directions, slots = agg_v.shape
    near_count, own = near_ref.shape
    adj_count = adj_ref.shape[1]
    list_len = list_ref.shape[0]
    surface = owner_ref.shape[1] // subs
    capacity = slots // devices
    per_tile = LANES // excites
    halves = boxes // per_tile
    unit = max(16, halves * capacity)
    amount = subs * surface
    all_rows = devices * unit
    my_dom = lax.axis_index("dom")
    my_dir = lax.axis_index("dir")
    me = my_dom * dirs + my_dir
    my_slot = my_dir * doms + my_dom
    right, left = lax.rem(my_dom + 1, doms), lax.rem(my_dom + doms - 1, doms)

    barrier = pltpu.get_barrier_semaphore()

    def greet(k, carry):
        other = lax.rem(me + k, devices)
        pl.semaphore_signal(
            barrier,
            inc=1,
            device_id=(lax.div(other, dirs), lax.rem(other, dirs)),
            device_id_type=MESH,
        )
        return carry

    lax.fori_loop(1, devices, greet, 0)

    locals_ = [
        pltpu.make_async_copy(src, dst, local_sem.at[i])
        for i, (src, dst) in enumerate(
            [
                (agg_hbm, agg_v),
                (trans_hbm, trans_t),
                (maps_hbm, maps_v),
                (coup_hbm, coup_v),
                (blocks_hbm, blocks_v),
            ]
        )
    ]
    schurs = [
        pltpu.make_async_copy(schur_hbm.at[s], schur_v.at[s], schur_sem.at[s]) for s in range(subs)
    ]
    locals_[0].start()
    schurs[0].start()
    schurs[1].start()
    locals_[4].start()
    for i in (1, 2, 3):
        locals_[i].start()
    for s in range(2, subs):
        schurs[s].start()

    owner_row = owner_ref[...]
    owner_col = jnp.concatenate(
        [
            jnp.broadcast_to(owner_row[:, k : k + LANES], (LANES, LANES)).T
            for k in range(0, amount, LANES)
        ],
        axis=0,
    )
    order = iota((amount, LANES), 0)
    ahead = order - iota((amount, LANES), 1)
    ranks = []
    for k in range(0, amount, LANES):
        same = (owner_col == owner_row[:, k : k + LANES]) & (ahead < k)
        ranks.append(jnp.sum(jnp.where(same, 1.0, 0.0), axis=0, keepdims=True))
    rank = jnp.concatenate(ranks, axis=1).astype(jnp.int32)
    half = (owner_row & (boxes - 1)) >> shift_of(per_tile)
    key = (owner_row >> shift_of(boxes)) * unit + half * capacity + rank
    place[...] = jnp.where(iota((doms * unit, amount), 0) == key, 1.0, 0.0).astype(BF16)
    wide = []
    for s in range(subs):
        piece = unk_ref[s][:, :surface].astype(F32)
        wide.append(jnp.concatenate([piece] * per_tile, axis=0).T)
    wide = jnp.concatenate(wide, axis=0)
    lane_box = iota((amount, LANES), 1) >> shift_of(excites)
    wide = jnp.where((owner_col & (per_tile - 1)) == lane_box, wide, 0.0).astype(BF16)
    send1[...] = dot(place[...], wide, 1, 0).astype(BF16)

    row = iota((all_rows, slots), 0)
    col = iota((all_rows, slots), 1)
    within = row & (unit - 1)
    slot_of = (row >> shift_of(unit)) * capacity + (within & (capacity - 1))
    for h in range(halves):
        hit = (slot_of == col) & ((within >> shift_of(capacity)) == h)
        perm[h] = jnp.where(hit, 1.0, 0.0).astype(BF16)

    pl.semaphore_wait(barrier, devices - 1)

    def tile(index):
        return pl.ds(pl.multiple_of(index * unit, unit), unit)

    def scatter(k, carry):
        other = lax.rem(me + k, devices)
        to_dom, to_dir = lax.div(other, dirs), lax.rem(other, dirs)
        pltpu.make_async_remote_copy(
            src_ref=send1.at[tile(to_dom)],
            dst_ref=recv1.at[tile(my_slot)],
            send_sem=send_sem.at[0],
            recv_sem=recv_sem.at[0],
            device_id=(to_dom, to_dir),
            device_id_type=MESH,
        ).start()
        return carry

    lax.fori_loop(1, devices, scatter, 0)
    recv1[tile(my_slot), :] = send1[tile(my_dom), :]

    sides = []
    for side, target in enumerate((right, left)):
        copy = pltpu.make_async_remote_copy(
            src_ref=unk_ref,
            dst_ref=recv0.at[side],
            send_sem=side_send.at[side],
            recv_sem=side_recv.at[side],
            device_id=(target, my_dir),
            device_id_type=MESH,
        )
        copy.start()
        sides.append(copy)

    def schur(s):
        schurs[s].wait()
        unknown = unk_ref[s]
        out_ref[s] = dot(unknown, schur_v[s], 1, 1)

    schur(0)
    schur(1)

    def drain(buffer, sem):
        size = pl.ds(0, all_rows - unit)
        pltpu.make_async_copy(buffer.at[size], buffer.at[size], sem).wait()

    drain(recv1, recv_sem.at[0])
    arrived = recv1[...]
    for h in range(halves):
        piece = dot(arrived, perm[h], 0, 0)
        curf[h * per_tile : (h + 1) * per_tile] = piece.reshape(per_tile, excites, slots)

    locals_[0].wait()
    chunks = 4
    chunk_boxes = boxes // chunks
    pair = 8
    wides = []
    for c in range(chunks):

        def radiate(i, carry):
            first = c * chunk_boxes + i * pair
            found = []
            for k in range(pair):
                b = first + k
                found.append(dot(curf[b].astype(BF16), agg_v[b], 1, 1))
            both = jnp.concatenate(found, axis=0).astype(BF16)
            size = pair * excites
            pats[pl.ds(pl.multiple_of(first * excites, size), size), :] = both
            patf[pl.ds(my_dom * boxes + first, pair)] = both.astype(F32).reshape(pair, excites, directions)
            return carry

        lax.fori_loop(0, chunk_boxes // pair, radiate, 0)
        at = pl.ds(c * chunk_boxes * excites, chunk_boxes * excites)
        for side, target in enumerate((right, left)):
            copy = pltpu.make_async_remote_copy(
                src_ref=pats.at[at],
                dst_ref=recv2.at[side, at],
                send_sem=wide_send.at[side, c],
                recv_sem=wide_recv.at[side, c],
                device_id=(target, my_dir),
                device_id_type=MESH,
            )
            copy.start()
            wides.append(copy)

    locals_[1].wait()
    trans_v[...] = trans_t[...].T

    locals_[4].wait()
    nearf[...] = jnp.zeros_like(nearf)

    near_pair = 4

    def near(i, carry):
        for k in range(near_pair):
            b = i * near_pair + k
            field = jnp.zeros((excites, slots), F32)
            for j in range(near_count):
                source = curf[near_ref[j, b]].astype(BF16)
                field = field + dot(source, blocks_v[b, j], 1, 1)
            nearf[my_dir * own + b] = field
        return carry

    lax.fori_loop(0, own // near_pair, near, 0)

    for copy in sides:
        copy.wait_recv()
    winf[0:subs] = recv0[0].astype(F32)
    winf[subs : 2 * subs] = unk_ref[...].astype(F32)
    winf[2 * subs : 3 * subs] = recv0[1].astype(F32)
    locals_[2].wait()
    locals_[3].wait()
    group_subs = subs * dirs
    sub_base = left * group_subs

    def couple(s, carry):
        fields = [jnp.zeros((excites, LANES), F32)] * (rows // LANES)
        for k in range(adj_count):
            offset = adj_ref[s, k] - sub_base
            offset = jnp.where(offset < 0, offset + group_subs * doms, offset)
            offset = jnp.minimum(offset, 3 * group_subs - 1)
            source = winf[lax.div(offset, group_subs) * subs + lax.rem(offset, subs)]
            mapping = maps_v[s, k : k + 1, :]
            factor = coup_v[s, k : k + 1, :]
            for c in range(rows // LANES):
                at = slice(c * LANES, (c + 1) * LANES)
                index = jnp.broadcast_to(mapping[:, at], (excites, LANES))
                low, high = index & (LANES - 1), index >> shift_of(LANES)
                value = jnp.zeros((excites, LANES), F32)
                for q in range(rows // LANES):
                    got = jnp.take_along_axis(
                        source[:, q * LANES : (q + 1) * LANES],
                        low,
                        axis=1,
                        mode="promise_in_bounds",
                    )
                    value = jnp.where(high == q, got, value)
                fields[c] = fields[c] + factor[:, at] * value
        coupled[s] = jnp.concatenate(fields, axis=1)
        return carry

    lax.fori_loop(0, subs, couple, 0)
    for s in range(2, subs - 1):
        schur(s)

    for copy in wides:
        copy.wait_recv()
    for side, source in enumerate((left, right)):
        patf[pl.ds(source * boxes, boxes)] = recv2[side].astype(F32).reshape(boxes, excites, directions)

    def respond(i, carry):
        first = i * pair
        found = []
        for k in range(pair):
            b = first + k
            field = jnp.zeros((excites, directions), F32)
            for j in range(list_len):
                field = field + trans_v[pl.ds(type_ref[j, b], 1), :] * patf[list_ref[j, b]]
            found.append(dot(field.astype(BF16), agg_v[b], 1, 0) + nearf[b])
        both = jnp.concatenate(found, axis=0).astype(BF16)
        size = pair * excites
        total[pl.ds(pl.multiple_of(first * excites, size), size), :] = both
        return carry

    lax.fori_loop(0, boxes // pair, respond, 0)
    leaving = jnp.zeros((all_rows, LANES), F32)
    for h in range(halves):
        leaving = leaving + dot(perm[h], total[h * LANES : (h + 1) * LANES, :], 1, 1)
    send3[...] = leaving.astype(BF16)

    def give_back(k, carry):
        other = lax.rem(me + k, devices)
        to_dom, to_dir = lax.div(other, dirs), lax.rem(other, dirs)
        pltpu.make_async_remote_copy(
            src_ref=send3.at[tile(to_dir * doms + to_dom)],
            dst_ref=recv3.at[tile(my_slot)],
            send_sem=send_sem.at[1],
            recv_sem=recv_sem.at[1],
            device_id=(to_dom, to_dir),
            device_id_type=MESH,
        ).start()
        return carry

    lax.fori_loop(1, devices, give_back, 0)
    recv3[tile(my_slot), :] = send3[tile(my_slot), :]

    schur(subs - 1)

    drain(recv3, recv_sem.at[1])
    group_rows = doms * unit
    field = jnp.zeros((group_rows, LANES), F32)
    for r in range(dirs):
        field = field + recv3[r * group_rows : (r + 1) * group_rows, :].astype(F32)
    back = dot(field.T.astype(BF16), place[...], 1, 0)
    sub_box = iota((LANES, amount), 0) >> shift_of(excites)
    back = jnp.where((owner_row & (per_tile - 1)) == sub_box, back, 0.0)
    back = jnp.sum(back.reshape(per_tile, excites, amount), axis=0)
    for s in range(subs):
        add = coupled[s]
        out_ref[s, :, :surface] += add[:, :surface] + back[:, s * surface : (s + 1) * surface]
        out_ref[s, :, surface:] += add[:, surface:]

    for copy in sides:
        copy.wait_send()
    for copy in wides:
        copy.wait_send()
    drain(recv1, send_sem.at[0])
    drain(recv3, send_sem.at[1])


def shards(
    mesh_dims,
    unknowns,
    schur_blocks,
    adjacency,
    row_map,
    coupling,
    owner_box,
    aggregation,
    trans_table,
    inter_list,
    inter_type,
    near_list,
    near_blocks,
):
    doms, dirs = mesh_dims
    subs, excites, rows = unknowns.shape
    boxes, slots, directions = aggregation.shape
    capacity = slots // (doms * dirs)
    per_tile = LANES // excites
    halves = boxes // per_tile
    unit = max(16, halves * capacity)
    all_rows = doms * dirs * unit
    amount = subs * owner_box.shape[1]
    vmem = pl.BlockSpec(memory_space=pltpu.VMEM)
    smem = pl.BlockSpec(memory_space=pltpu.SMEM)
    hbm = pl.BlockSpec(memory_space=pl.ANY)
    dma = pltpu.SemaphoreType.DMA
    scratch = [
        pltpu.VMEM((boxes, directions, slots), BF16),
        pltpu.VMEM(trans_table.shape, F32),
        pltpu.VMEM(trans_table.shape[::-1], F32),
        pltpu.VMEM(row_map.shape, jnp.int32),
        pltpu.VMEM(coupling.shape, F32),
        pltpu.VMEM(schur_blocks.shape, BF16),
        pltpu.VMEM(near_blocks.shape, BF16),
        pltpu.VMEM((doms * unit, amount), BF16),
        pltpu.VMEM((halves, all_rows, slots), BF16),
        pltpu.VMEM((doms * unit, LANES), BF16),
        pltpu.VMEM((all_rows, LANES), BF16),
        pltpu.VMEM((2, subs, excites, rows), BF16),
        pltpu.VMEM((3 * subs, excites, rows), F32),
        pltpu.VMEM((boxes, excites, slots), F32),
        pltpu.VMEM((boxes * excites, directions), BF16),
        pltpu.VMEM((2, boxes * excites, directions), BF16),
        pltpu.VMEM((doms * boxes, excites, directions), F32),
        pltpu.VMEM((subs, excites, rows), F32),
        pltpu.VMEM((boxes, excites, slots), F32),
        pltpu.VMEM((boxes * excites, slots), BF16),
        pltpu.VMEM((all_rows, LANES), BF16),
        pltpu.VMEM((all_rows, LANES), BF16),
        dma((5,)),
        dma((subs,)),
        dma((2,)),
        dma((2,)),
        dma((2,)),
        dma((2,)),
        dma((2, 4)),
        dma((2, 4)),
    ]
    return pl.pallas_call(
        functools.partial(kernel, mesh_dims),
        out_shape=jax.ShapeDtypeStruct(unknowns.shape, F32),
        in_specs=[smem] * 4 + [vmem] * 2 + [hbm] * 6,
        out_specs=vmem,
        scratch_shapes=scratch,
        compiler_params=pltpu.CompilerParams(
            collective_id=0, has_side_effects=True, vmem_limit_bytes=52 * 1024 * 1024
        ),
    )(
        adjacency,
        inter_list.T,
        inter_type.T,
        near_list.T,
        unknowns,
        owner_box.reshape(1, amount),
        jnp.swapaxes(aggregation, 1, 2),
        trans_table.T,
        row_map,
        coupling,
        schur_blocks,
        near_blocks,
    )


def solution(mesh):
    in_specs = (
        P(("dom", "dir"), None, None),
        P(("dom", "dir"), None, None),
        P(("dom", "dir"), None),
        P(("dom", "dir"), None, None),
        P(("dom", "dir"), None, None),
        P(("dom", "dir"), None, None),
        P("dom", None, "dir"),
        P(None, "dir"),
        P("dom", None),
        P("dom", None),
        P(("dom", "dir"), None),
        P(("dom", "dir"), None, None, None),
    )
    out_specs = P(("dom", "dir"), None, None)
    dims = (mesh.shape["dom"], mesh.shape["dir"])
    return jax.shard_map(
        functools.partial(shards, dims),
        mesh=mesh,
        in_specs=in_specs,
        out_specs=out_specs,
        check_vma=False,
    )
```

```python
import functools

import jax
import jax.numpy as jnp
from jax import lax
from jax.experimental import pallas as pl
from jax.experimental.pallas import tpu as pltpu
from jax.sharding import PartitionSpec as P

MESH = pl.DeviceIdType.MESH
LANES = 128
F32 = jnp.float32
BF16 = jnp.bfloat16


def dot(a, b, ca, cb):
    return lax.dot_general(a, b, (((ca,), (cb,)), ((), ())), preferred_element_type=F32)


def iota(shape, dim):
    return lax.broadcasted_iota(jnp.int32, shape, dim)


def shift_of(value):
    bits = value.bit_length() - 1
    assert value == 1 << bits
    return bits


def kernel(
    dims,
    adj_hbm,
    list_hbm,
    type_hbm,
    near_hbm,
    unk_ref,
    owner_ref,
    agg_hbm,
    trans_hbm,
    maps_hbm,
    coup_hbm,
    schur_hbm,
    blocks_hbm,
    out_ref,
    adj_ref,
    list_ref,
    type_ref,
    near_ref,
    agg_v,
    trans_v,
    trans_t,
    maps_v,
    coup_v,
    schur_v,
    blocks_v,
    place,
    perm,
    send1,
    recv1,
    recv0,
    winf,
    curf,
    pats,
    recv2,
    patf,
    coupled,
    nearf,
    total,
    send3,
    recv3,
    local_sem,
    schur_sem,
    send_sem,
    recv_sem,
    side_send,
    side_recv,
    wide_send,
    wide_recv,
):
    doms, dirs = dims
    devices = doms * dirs
    subs, excites, rows = unk_ref.shape
    boxes, directions, slots = agg_v.shape
    near_count, own = near_ref.shape
    adj_count = adj_ref.shape[1]
    list_len = list_ref.shape[0]
    surface = owner_ref.shape[1] // subs
    capacity = slots // devices
    per_tile = LANES // excites
    halves = boxes // per_tile
    unit = max(16, halves * capacity)
    amount = subs * surface
    all_rows = devices * unit
    my_dom = lax.axis_index("dom")
    my_dir = lax.axis_index("dir")
    me = my_dom * dirs + my_dir
    my_slot = my_dir * doms + my_dom
    right, left = lax.rem(my_dom + 1, doms), lax.rem(my_dom + doms - 1, doms)
    odd = lax.rem(my_dom, 2)
    partner = my_dom + 1 - 2 * odd
    relay_to = lax.rem(my_dom + 2 - 4 * odd + doms, doms)
    relay_from = lax.rem(my_dom - 2 + 4 * odd + doms, doms)
    relay_source = relay_from + 1 - 2 * odd

    barrier = pltpu.get_barrier_semaphore()

    def greet(k, carry):
        other = lax.rem(me + k, devices)
        pl.semaphore_signal(
            barrier,
            inc=1,
            device_id=(lax.div(other, dirs), lax.rem(other, dirs)),
            device_id_type=MESH,
        )
        return carry

    lax.fori_loop(1, devices, greet, 0)

    locals_ = [
        pltpu.make_async_copy(src, dst, local_sem.at[i])
        for i, (src, dst) in enumerate(
            [
                (agg_hbm, agg_v),
                (trans_hbm, trans_t),
                (maps_hbm, maps_v),
                (coup_hbm, coup_v),
                (blocks_hbm, blocks_v),
                (adj_hbm, adj_ref),
                (list_hbm, list_ref),
                (type_hbm, type_ref),
                (near_hbm, near_ref),
            ]
        )
    ]
    schurs = [
        pltpu.make_async_copy(schur_hbm.at[s], schur_v.at[s], schur_sem.at[s]) for s in range(subs)
    ]
    locals_[0].start()
    schurs[0].start()
    schurs[1].start()
    locals_[4].start()
    for i in (1, 2, 3, 5, 6, 7, 8):
        locals_[i].start()
    for s in range(2, subs):
        schurs[s].start()

    owner_row = owner_ref[...]
    owner_col = jnp.concatenate(
        [
            jnp.broadcast_to(owner_row[:, k : k + LANES], (LANES, LANES)).T
            for k in range(0, amount, LANES)
        ],
        axis=0,
    )
    order = iota((amount, LANES), 0)
    ahead = order - iota((amount, LANES), 1)
    ranks = []
    for k in range(0, amount, LANES):
        same = (owner_col == owner_row[:, k : k + LANES]) & (ahead < k)
        ranks.append(jnp.sum(jnp.where(same, 1.0, 0.0), axis=0, keepdims=True))
    rank = jnp.concatenate(ranks, axis=1).astype(jnp.int32)
    half = (owner_row & (boxes - 1)) >> shift_of(per_tile)
    key = (owner_row >> shift_of(boxes)) * unit + half * capacity + rank
    place[...] = jnp.where(iota((doms * unit, amount), 0) == key, 1.0, 0.0).astype(BF16)
    wide = []
    for s in range(subs):
        piece = unk_ref[s][:, :surface].astype(F32)
        wide.append(jnp.concatenate([piece] * per_tile, axis=0).T)
    wide = jnp.concatenate(wide, axis=0)
    lane_box = iota((amount, LANES), 1) >> shift_of(excites)
    wide = jnp.where((owner_col & (per_tile - 1)) == lane_box, wide, 0.0).astype(BF16)
    send1[...] = dot(place[...], wide, 1, 0).astype(BF16)

    row = iota((all_rows, slots), 0)
    col = iota((all_rows, slots), 1)
    within = row & (unit - 1)
    slot_of = (row >> shift_of(unit)) * capacity + (within & (capacity - 1))
    for h in range(halves):
        hit = (slot_of == col) & ((within >> shift_of(capacity)) == h)
        perm[h] = jnp.where(hit, 1.0, 0.0).astype(BF16)

    pl.semaphore_wait(barrier, devices - 1)

    def tile(index):
        return pl.ds(pl.multiple_of(index * unit, unit), unit)

    def scatter(k, carry):
        other = lax.rem(me + k, devices)
        to_dom, to_dir = lax.div(other, dirs), lax.rem(other, dirs)
        pltpu.make_async_remote_copy(
            src_ref=send1.at[tile(to_dom)],
            dst_ref=recv1.at[tile(my_slot)],
            send_sem=send_sem.at[0],
            recv_sem=recv_sem.at[0],
            device_id=(to_dom, to_dir),
            device_id_type=MESH,
        ).start()
        return carry

    lax.fori_loop(1, devices, scatter, 0)
    recv1[tile(my_slot), :] = send1[tile(my_dom), :]

    sides = []
    for side, target in enumerate((right, left)):
        copy = pltpu.make_async_remote_copy(
            src_ref=unk_ref,
            dst_ref=recv0.at[side],
            send_sem=side_send.at[side],
            recv_sem=side_recv.at[side],
            device_id=(target, my_dir),
            device_id_type=MESH,
        )
        copy.start()
        sides.append(copy)

    def schur(s):
        schurs[s].wait()
        unknown = unk_ref[s]
        out_ref[s] = dot(unknown, schur_v[s], 1, 1)

    schur(0)
    schur(1)

    def drain(buffer, sem):
        size = pl.ds(0, all_rows - unit)
        pltpu.make_async_copy(buffer.at[size], buffer.at[size], sem).wait()

    drain(recv1, recv_sem.at[0])
    arrived = recv1[...]
    for h in range(halves):
        piece = dot(arrived, perm[h], 0, 0)
        curf[h * per_tile : (h + 1) * per_tile] = piece.reshape(per_tile, excites, slots)

    locals_[0].wait()
    chunks = 4
    chunk_boxes = boxes // chunks
    pair = 8
    wides = []
    for c in range(chunks):

        def radiate(i, carry):
            first = c * chunk_boxes + i * pair
            found = []
            for k in range(pair):
                b = first + k
                found.append(dot(curf[b].astype(BF16), agg_v[b], 1, 1))
            both = jnp.concatenate(found, axis=0).astype(BF16)
            size = pair * excites
            pats[pl.ds(pl.multiple_of(first * excites, size), size), :] = both
            patf[pl.ds(my_dom * boxes + first, pair)] = both.astype(F32).reshape(pair, excites, directions)
            return carry

        lax.fori_loop(0, chunk_boxes // pair, radiate, 0)
        at = pl.ds(c * chunk_boxes * excites, chunk_boxes * excites)
        copy = pltpu.make_async_remote_copy(
            src_ref=pats.at[at],
            dst_ref=recv2.at[0, at],
            send_sem=wide_send.at[0, c],
            recv_sem=wide_recv.at[0, c],
            device_id=(partner, my_dir),
            device_id_type=MESH,
        )
        copy.start()
        wides.append(copy)

    relays = []

    def relay(c):
        wides[c].wait_recv()
        at = pl.ds(c * chunk_boxes * excites, chunk_boxes * excites)
        copy = pltpu.make_async_remote_copy(
            src_ref=recv2.at[0, at],
            dst_ref=recv2.at[1, at],
            send_sem=wide_send.at[1, c],
            recv_sem=wide_recv.at[1, c],
            device_id=(relay_to, my_dir),
            device_id_type=MESH,
        )
        copy.start()
        relays.append(copy)

    for i in (1, 2, 3, 5, 6, 7, 8):
        locals_[i].wait()
    trans_v[...] = trans_t[...].T

    locals_[4].wait()
    nearf[...] = jnp.zeros_like(nearf)

    def near(b):
        field = jnp.zeros((excites, slots), F32)
        for j in range(near_count):
            source = curf[near_ref[j, b]].astype(BF16)
            field = field + dot(source, blocks_v[b, j], 1, 1)
        nearf[my_dir * own + b] = field

    relay(0)
    for b in range(own // 2):
        near(b)
    relay(1)
    for b in range(own // 2, own):
        near(b)
    relay(2)

    for copy in sides:
        copy.wait_recv()
    winf[0:subs] = recv0[0].astype(F32)
    winf[subs : 2 * subs] = unk_ref[...].astype(F32)
    winf[2 * subs : 3 * subs] = recv0[1].astype(F32)
    relay(3)
    group_subs = subs * dirs
    sub_base = left * group_subs

    def couple(s, carry):
        fields = [jnp.zeros((excites, LANES), F32)] * (rows // LANES)
        for k in range(adj_count):
            offset = adj_ref[s, k] - sub_base
            offset = jnp.where(offset < 0, offset + group_subs * doms, offset)
            offset = jnp.minimum(offset, 3 * group_subs - 1)
            source = winf[lax.div(offset, group_subs) * subs + lax.rem(offset, subs)]
            mapping = maps_v[s, k : k + 1, :]
            factor = coup_v[s, k : k + 1, :]
            for c in range(rows // LANES):
                at = slice(c * LANES, (c + 1) * LANES)
                index = jnp.broadcast_to(mapping[:, at], (excites, LANES))
                low, high = index & (LANES - 1), index >> shift_of(LANES)
                value = jnp.zeros((excites, LANES), F32)
                for q in range(rows // LANES):
                    got = jnp.take_along_axis(
                        source[:, q * LANES : (q + 1) * LANES],
                        low,
                        axis=1,
                        mode="promise_in_bounds",
                    )
                    value = jnp.where(high == q, got, value)
                fields[c] = fields[c] + factor[:, at] * value
        coupled[s] = jnp.concatenate(fields, axis=1)
        return carry

    lax.fori_loop(0, subs, couple, 0)
    for s in range(2, subs - 1):
        schur(s)

    for copy in relays:
        copy.wait_recv()
    for side, source in enumerate((partner, relay_source)):
        patf[pl.ds(source * boxes, boxes)] = recv2[side].astype(F32).reshape(boxes, excites, directions)

    def respond(i, carry):
        first = i * pair
        found = []
        for k in range(pair):
            b = first + k
            field = jnp.zeros((excites, directions), F32)
            for j in range(list_len):
                field = field + trans_v[pl.ds(type_ref[j, b], 1), :] * patf[list_ref[j, b]]
            found.append(dot(field.astype(BF16), agg_v[b], 1, 0) + nearf[b])
        both = jnp.concatenate(found, axis=0).astype(BF16)
        size = pair * excites
        total[pl.ds(pl.multiple_of(first * excites, size), size), :] = both
        return carry

    lax.fori_loop(0, boxes // pair, respond, 0)
    leaving = jnp.zeros((all_rows, LANES), F32)
    for h in range(halves):
        leaving = leaving + dot(perm[h], total[h * LANES : (h + 1) * LANES, :], 1, 1)
    send3[...] = leaving.astype(BF16)

    def give_back(k, carry):
        other = lax.rem(me + k, devices)
        to_dom, to_dir = lax.div(other, dirs), lax.rem(other, dirs)
        pltpu.make_async_remote_copy(
            src_ref=send3.at[tile(to_dir * doms + to_dom)],
            dst_ref=recv3.at[tile(my_slot)],
            send_sem=send_sem.at[1],
            recv_sem=recv_sem.at[1],
            device_id=(to_dom, to_dir),
            device_id_type=MESH,
        ).start()
        return carry

    lax.fori_loop(1, devices, give_back, 0)
    recv3[tile(my_slot), :] = send3[tile(my_slot), :]

    schur(subs - 1)

    drain(recv3, recv_sem.at[1])
    group_rows = doms * unit
    field = jnp.zeros((group_rows, LANES), F32)
    for r in range(dirs):
        field = field + recv3[r * group_rows : (r + 1) * group_rows, :].astype(F32)
    back = dot(field.T.astype(BF16), place[...], 1, 0)
    sub_box = iota((LANES, amount), 0) >> shift_of(excites)
    back = jnp.where((owner_row & (per_tile - 1)) == sub_box, back, 0.0)
    back = jnp.sum(back.reshape(per_tile, excites, amount), axis=0)
    for s in range(subs):
        add = coupled[s]
        out_ref[s, :, :surface] += add[:, :surface] + back[:, s * surface : (s + 1) * surface]
        out_ref[s, :, surface:] += add[:, surface:]

    for copy in sides:
        copy.wait_send()
    for copy in wides + relays:
        copy.wait_send()
    drain(recv1, send_sem.at[0])
    drain(recv3, send_sem.at[1])


def shards(
    mesh_dims,
    unknowns,
    schur_blocks,
    adjacency,
    row_map,
    coupling,
    owner_box,
    aggregation,
    trans_table,
    inter_list,
    inter_type,
    near_list,
    near_blocks,
):
    doms, dirs = mesh_dims
    subs, excites, rows = unknowns.shape
    boxes, slots, directions = aggregation.shape
    capacity = slots // (doms * dirs)
    per_tile = LANES // excites
    halves = boxes // per_tile
    unit = max(16, halves * capacity)
    all_rows = doms * dirs * unit
    amount = subs * owner_box.shape[1]
    vmem = pl.BlockSpec(memory_space=pltpu.VMEM)
    hbm = pl.BlockSpec(memory_space=pl.ANY)
    dma = pltpu.SemaphoreType.DMA
    smem = [
        pltpu.SMEM(value.shape, jnp.int32)
        for value in (adjacency, inter_list.T, inter_type.T, near_list.T)
    ]
    scratch = smem + [
        pltpu.VMEM((boxes, directions, slots), BF16),
        pltpu.VMEM(trans_table.shape, F32),
        pltpu.VMEM(trans_table.shape[::-1], F32),
        pltpu.VMEM(row_map.shape, jnp.int32),
        pltpu.VMEM(coupling.shape, F32),
        pltpu.VMEM(schur_blocks.shape, BF16),
        pltpu.VMEM(near_blocks.shape, BF16),
        pltpu.VMEM((doms * unit, amount), BF16),
        pltpu.VMEM((halves, all_rows, slots), BF16),
        pltpu.VMEM((doms * unit, LANES), BF16),
        pltpu.VMEM((all_rows, LANES), BF16),
        pltpu.VMEM((2, subs, excites, rows), BF16),
        pltpu.VMEM((3 * subs, excites, rows), F32),
        pltpu.VMEM((boxes, excites, slots), F32),
        pltpu.VMEM((boxes * excites, directions), BF16),
        pltpu.VMEM((2, boxes * excites, directions), BF16),
        pltpu.VMEM((doms * boxes, excites, directions), F32),
        pltpu.VMEM((subs, excites, rows), F32),
        pltpu.VMEM((boxes, excites, slots), F32),
        pltpu.VMEM((boxes * excites, slots), BF16),
        pltpu.VMEM((all_rows, LANES), BF16),
        pltpu.VMEM((all_rows, LANES), BF16),
        dma((9,)),
        dma((subs,)),
        dma((2,)),
        dma((2,)),
        dma((2,)),
        dma((2,)),
        dma((2, 4)),
        dma((2, 4)),
    ]
    return pl.pallas_call(
        functools.partial(kernel, mesh_dims),
        out_shape=pltpu.VMEM(unknowns.shape, F32),
        in_specs=[hbm] * 4 + [vmem] * 2 + [hbm] * 6,
        out_specs=vmem,
        scratch_shapes=scratch,
        compiler_params=pltpu.CompilerParams(
            collective_id=0, has_side_effects=True, vmem_limit_bytes=56 * 1024 * 1024
        ),
    )(
        adjacency,
        inter_list.T,
        inter_type.T,
        near_list.T,
        unknowns,
        owner_box.reshape(1, amount),
        jnp.swapaxes(aggregation, 1, 2),
        trans_table.T,
        row_map,
        coupling,
        schur_blocks,
        near_blocks,
    )


def solution(mesh):
    in_specs = (
        P(("dom", "dir"), None, None),
        P(("dom", "dir"), None, None),
        P(("dom", "dir"), None),
        P(("dom", "dir"), None, None),
        P(("dom", "dir"), None, None),
        P(("dom", "dir"), None, None),
        P("dom", None, "dir"),
        P(None, "dir"),
        P("dom", None),
        P("dom", None),
        P(("dom", "dir"), None),
        P(("dom", "dir"), None, None, None),
    )
    out_specs = P(("dom", "dir"), None, None)
    dims = (mesh.shape["dom"], mesh.shape["dir"])
    return jax.shard_map(
        functools.partial(shards, dims),
        mesh=mesh,
        in_specs=in_specs,
        out_specs=out_specs,
        check_vma=False,
    )
```

```python
import functools

import jax
import jax.numpy as jnp
from jax import lax
from jax.experimental import pallas as pl
from jax.experimental.pallas import tpu as pltpu
from jax.sharding import PartitionSpec as P

MESH = pl.DeviceIdType.MESH
LANES = 128
F32 = jnp.float32
BF16 = jnp.bfloat16


def dot(a, b, ca, cb):
    return lax.dot_general(a, b, (((ca,), (cb,)), ((), ())), preferred_element_type=F32)


def iota(shape, dim):
    return lax.broadcasted_iota(jnp.int32, shape, dim)


def shift_of(value):
    bits = value.bit_length() - 1
    assert value == 1 << bits
    return bits


def kernel(
    dims,
    adj_hbm,
    list_hbm,
    type_hbm,
    near_hbm,
    unk_ref,
    owner_ref,
    agg_hbm,
    trans_hbm,
    maps_hbm,
    coup_hbm,
    schur_hbm,
    blocks_hbm,
    out_ref,
    adj_ref,
    list_ref,
    type_ref,
    near_ref,
    agg_v,
    trans_v,
    trans_t,
    maps_v,
    coup_v,
    schur_v,
    blocks_v,
    place,
    perm,
    send1,
    recv1,
    recv0,
    winf,
    curf,
    pats,
    recv2,
    patf,
    coupled,
    nearf,
    total,
    send3,
    recv3,
    local_sem,
    schur_sem,
    send_sem,
    recv_sem,
    side_send,
    side_recv,
    wide_send,
    wide_recv,
):
    doms, dirs = dims
    devices = doms * dirs
    subs, excites, rows = unk_ref.shape
    boxes, directions, slots = agg_v.shape
    near_count, own = near_ref.shape
    adj_count = adj_ref.shape[1]
    list_len = list_ref.shape[0]
    surface = owner_ref.shape[1] // subs
    capacity = slots // devices
    per_tile = LANES // excites
    halves = boxes // per_tile
    unit = max(16, halves * capacity)
    amount = subs * surface
    all_rows = devices * unit
    my_dom = lax.axis_index("dom")
    my_dir = lax.axis_index("dir")
    me = my_dom * dirs + my_dir
    my_slot = my_dir * doms + my_dom
    right, left = lax.rem(my_dom + 1, doms), lax.rem(my_dom + doms - 1, doms)
    odd = lax.rem(my_dom, 2)
    partner = my_dom + 1 - 2 * odd
    relay_to = lax.rem(my_dom + 2 - 4 * odd + doms, doms)
    relay_from = lax.rem(my_dom - 2 + 4 * odd + doms, doms)
    relay_source = relay_from + 1 - 2 * odd

    barrier = pltpu.get_barrier_semaphore()

    def greet(k, carry):
        other = lax.rem(me + k, devices)
        pl.semaphore_signal(
            barrier,
            inc=1,
            device_id=(lax.div(other, dirs), lax.rem(other, dirs)),
            device_id_type=MESH,
        )
        return carry

    lax.fori_loop(1, devices, greet, 0)

    locals_ = [
        pltpu.make_async_copy(src, dst, local_sem.at[i])
        for i, (src, dst) in enumerate(
            [
                (agg_hbm, agg_v),
                (trans_hbm, trans_t),
                (maps_hbm, maps_v),
                (coup_hbm, coup_v),
                (blocks_hbm, blocks_v),
                (adj_hbm, adj_ref),
                (list_hbm, list_ref),
                (type_hbm, type_ref),
                (near_hbm, near_ref),
            ]
        )
    ]
    schurs = [
        pltpu.make_async_copy(schur_hbm.at[s], schur_v.at[s], schur_sem.at[s]) for s in range(subs)
    ]
    locals_[0].start()
    schurs[0].start()
    schurs[1].start()
    locals_[1].start()

    owner_row = owner_ref[...]
    owner_col = jnp.concatenate(
        [
            jnp.broadcast_to(owner_row[:, k : k + LANES], (LANES, LANES)).T
            for k in range(0, amount, LANES)
        ],
        axis=0,
    )
    ahead = iota((LANES, LANES), 0) < iota((LANES, LANES), 1)
    ranks = []
    for k in range(0, amount, LANES):
        piece = owner_row[:, k : k + LANES]
        same = (owner_col[k : k + LANES] == piece) & ahead
        count = jnp.sum(jnp.where(same, 1.0, 0.0), axis=0, keepdims=True)
        if k > 0:
            earlier = jnp.where(owner_col[:k] == piece, 1.0, 0.0)
            count = count + jnp.sum(earlier, axis=0, keepdims=True)
        ranks.append(count)
    rank = jnp.concatenate(ranks, axis=1).astype(jnp.int32)
    half = (owner_row & (boxes - 1)) >> shift_of(per_tile)
    key = (owner_row >> shift_of(boxes)) * unit + half * capacity + rank
    place[...] = jnp.where(iota((doms * unit, amount), 0) == key, 1.0, 0.0).astype(BF16)
    wide = []
    for s in range(subs):
        piece = unk_ref[s][:, :surface].astype(F32)
        wide.append(jnp.concatenate([piece] * per_tile, axis=0).T)
    wide = jnp.concatenate(wide, axis=0)
    lane_box = iota((amount, LANES), 1) >> shift_of(excites)
    wide = jnp.where((owner_col & (per_tile - 1)) == lane_box, wide, 0.0).astype(BF16)
    send1[...] = dot(place[...], wide, 1, 0).astype(BF16)

    pl.semaphore_wait(barrier, devices - 1)

    def tile(index):
        return pl.ds(pl.multiple_of(index * unit, unit), unit)

    def scatter(k, carry):
        other = lax.rem(me + k, devices)
        to_dom, to_dir = lax.div(other, dirs), lax.rem(other, dirs)
        pltpu.make_async_remote_copy(
            src_ref=send1.at[tile(to_dom)],
            dst_ref=recv1.at[tile(my_slot)],
            send_sem=send_sem.at[0],
            recv_sem=recv_sem.at[0],
            device_id=(to_dom, to_dir),
            device_id_type=MESH,
        ).start()
        return carry

    lax.fori_loop(1, devices, scatter, 0)
    recv1[tile(my_slot), :] = send1[tile(my_dom), :]

    locals_[4].start()
    for s in range(2, subs):
        schurs[s].start()
    for i in (2, 3, 5, 6, 7, 8):
        locals_[i].start()

    row = iota((all_rows, slots), 0)
    col = iota((all_rows, slots), 1)
    within = row & (unit - 1)
    slot_of = (row >> shift_of(unit)) * capacity + (within & (capacity - 1))
    for h in range(halves):
        hit = (slot_of == col) & ((within >> shift_of(capacity)) == h)
        perm[h] = jnp.where(hit, 1.0, 0.0).astype(BF16)

    def schur(s):
        schurs[s].wait()
        unknown = unk_ref[s]
        out_ref[s] = dot(unknown, schur_v[s], 1, 1)

    schur(0)
    schur(1)
    locals_[1].wait()
    turned = trans_t[...].T
    trans_v[...] = jnp.broadcast_to(
        turned[:, None, :], (turned.shape[0], excites, turned.shape[1])
    )

    def drain(buffer, sem):
        size = pl.ds(0, all_rows - unit)
        pltpu.make_async_copy(buffer.at[size], buffer.at[size], sem).wait()

    drain(recv1, recv_sem.at[0])
    arrived = recv1[...]
    for h in range(halves):
        piece = dot(arrived, perm[h], 0, 0)
        curf[h * per_tile : (h + 1) * per_tile] = piece.reshape(per_tile, excites, slots)

    locals_[0].wait()
    chunks = 4
    chunk_boxes = boxes // chunks
    pair = 8
    wides = []
    for c in range(chunks):

        def radiate(i, carry):
            first = c * chunk_boxes + i * pair
            found = []
            for k in range(pair):
                b = first + k
                found.append(dot(curf[b].astype(BF16), agg_v[b], 1, 1))
            both = jnp.concatenate(found, axis=0).astype(BF16)
            size = pair * excites
            pats[pl.ds(pl.multiple_of(first * excites, size), size), :] = both
            patf[pl.ds(my_dom * boxes + first, pair)] = both.astype(F32).reshape(pair, excites, directions)
            return carry

        lax.fori_loop(0, chunk_boxes // pair, radiate, 0)
        at = pl.ds(c * chunk_boxes * excites, chunk_boxes * excites)
        copy = pltpu.make_async_remote_copy(
            src_ref=pats.at[at],
            dst_ref=recv2.at[0, at],
            send_sem=wide_send.at[0, c],
            recv_sem=wide_recv.at[0, c],
            device_id=(partner, my_dir),
            device_id_type=MESH,
        )
        copy.start()
        wides.append(copy)

    sides = []
    for side, target in enumerate((right, left)):
        copy = pltpu.make_async_remote_copy(
            src_ref=unk_ref,
            dst_ref=recv0.at[side],
            send_sem=side_send.at[side],
            recv_sem=side_recv.at[side],
            device_id=(target, my_dir),
            device_id_type=MESH,
        )
        copy.start()
        sides.append(copy)

    relays = []

    def relay(c):
        wides[c].wait_recv()
        at = pl.ds(c * chunk_boxes * excites, chunk_boxes * excites)
        copy = pltpu.make_async_remote_copy(
            src_ref=recv2.at[0, at],
            dst_ref=recv2.at[1, at],
            send_sem=wide_send.at[1, c],
            recv_sem=wide_recv.at[1, c],
            device_id=(relay_to, my_dir),
            device_id_type=MESH,
        )
        copy.start()
        relays.append(copy)

    for i in (2, 3, 5, 6, 7, 8):
        locals_[i].wait()

    locals_[4].wait()
    nearf[...] = jnp.zeros_like(nearf)

    def near(b):
        field = jnp.zeros((excites, slots), F32)
        for j in range(near_count):
            source = curf[near_ref[j, b]].astype(BF16)
            field = field + dot(source, blocks_v[b, j], 1, 1)
        nearf[my_dir * own + b] = field

    relay(0)
    for b in range(own):
        near(b)
        if b + 1 in (own // 2, own * 3 // 4, own):
            relay((own // 2, own * 3 // 4, own).index(b + 1) + 1)
    for s in range(2, subs - 1):
        schur(s)

    for copy in relays:
        copy.wait_recv()
    for side, source in enumerate((partner, relay_source)):
        patf[pl.ds(source * boxes, boxes)] = recv2[side].astype(F32).reshape(boxes, excites, directions)

    def respond(i, carry):
        first = i * pair
        found = []
        for k in range(pair):
            b = first + k
            field = jnp.zeros((excites, directions), F32)
            for j in range(list_len):
                field = field + trans_v[type_ref[j, b]] * patf[list_ref[j, b]]
            found.append(dot(field.astype(BF16), agg_v[b], 1, 0) + nearf[b])
        both = jnp.concatenate(found, axis=0).astype(BF16)
        size = pair * excites
        total[pl.ds(pl.multiple_of(first * excites, size), size), :] = both
        return carry

    lax.fori_loop(0, boxes // pair, respond, 0)
    leaving = jnp.zeros((all_rows, LANES), F32)
    for h in range(halves):
        leaving = leaving + dot(perm[h], total[h * LANES : (h + 1) * LANES, :], 1, 1)
    send3[...] = leaving.astype(BF16)

    def give_back(k, carry):
        other = lax.rem(me + k, devices)
        to_dom, to_dir = lax.div(other, dirs), lax.rem(other, dirs)
        pltpu.make_async_remote_copy(
            src_ref=send3.at[tile(to_dir * doms + to_dom)],
            dst_ref=recv3.at[tile(my_slot)],
            send_sem=send_sem.at[1],
            recv_sem=recv_sem.at[1],
            device_id=(to_dom, to_dir),
            device_id_type=MESH,
        ).start()
        return carry

    lax.fori_loop(1, devices, give_back, 0)
    recv3[tile(my_slot), :] = send3[tile(my_slot), :]

    schur(subs - 1)

    for copy in sides:
        copy.wait_recv()
    winf[0:subs] = recv0[0].astype(F32)
    winf[subs : 2 * subs] = unk_ref[...].astype(F32)
    winf[2 * subs : 3 * subs] = recv0[1].astype(F32)
    group_subs = subs * dirs
    sub_base = left * group_subs

    def couple(s, carry):
        fields = [jnp.zeros((excites, LANES), F32)] * (rows // LANES)
        for k in range(adj_count):
            offset = adj_ref[s, k] - sub_base
            offset = jnp.where(offset < 0, offset + group_subs * doms, offset)
            offset = jnp.minimum(offset, 3 * group_subs - 1)
            source = winf[lax.div(offset, group_subs) * subs + lax.rem(offset, subs)]
            mapping = maps_v[s, k : k + 1, :]
            factor = coup_v[s, k : k + 1, :]
            for c in range(rows // LANES):
                at = slice(c * LANES, (c + 1) * LANES)
                index = jnp.broadcast_to(mapping[:, at], (excites, LANES))
                low, high = index & (LANES - 1), index >> shift_of(LANES)
                value = jnp.zeros((excites, LANES), F32)
                for q in range(rows // LANES):
                    got = jnp.take_along_axis(
                        source[:, q * LANES : (q + 1) * LANES],
                        low,
                        axis=1,
                        mode="promise_in_bounds",
                    )
                    value = jnp.where(high == q, got, value)
                fields[c] = fields[c] + factor[:, at] * value
        coupled[s] = jnp.concatenate(fields, axis=1)
        return carry

    lax.fori_loop(0, subs, couple, 0)

    drain(recv3, recv_sem.at[1])
    group_rows = doms * unit
    field = jnp.zeros((group_rows, LANES), F32)
    for r in range(dirs):
        field = field + recv3[r * group_rows : (r + 1) * group_rows, :].astype(F32)
    back = dot(field.T.astype(BF16), place[...], 1, 0)
    sub_box = iota((LANES, amount), 0) >> shift_of(excites)
    back = jnp.where((owner_row & (per_tile - 1)) == sub_box, back, 0.0)
    back = jnp.sum(back.reshape(per_tile, excites, amount), axis=0)
    for s in range(subs):
        add = coupled[s]
        out_ref[s, :, :surface] += add[:, :surface] + back[:, s * surface : (s + 1) * surface]
        out_ref[s, :, surface:] += add[:, surface:]

    for copy in sides:
        copy.wait_send()
    for copy in wides + relays:
        copy.wait_send()
    drain(recv1, send_sem.at[0])
    drain(recv3, send_sem.at[1])


def shards(
    mesh_dims,
    unknowns,
    schur_blocks,
    adjacency,
    row_map,
    coupling,
    owner_box,
    aggregation,
    trans_table,
    inter_list,
    inter_type,
    near_list,
    near_blocks,
):
    doms, dirs = mesh_dims
    subs, excites, rows = unknowns.shape
    boxes, slots, directions = aggregation.shape
    capacity = slots // (doms * dirs)
    per_tile = LANES // excites
    halves = boxes // per_tile
    unit = max(16, halves * capacity)
    all_rows = doms * dirs * unit
    amount = subs * owner_box.shape[1]
    vmem = pl.BlockSpec(memory_space=pltpu.VMEM)
    hbm = pl.BlockSpec(memory_space=pl.ANY)
    dma = pltpu.SemaphoreType.DMA
    smem = [
        pltpu.SMEM(value.shape, jnp.int32)
        for value in (adjacency, inter_list.T, inter_type.T, near_list.T)
    ]
    scratch = smem + [
        pltpu.VMEM((boxes, directions, slots), BF16),
        pltpu.VMEM((trans_table.shape[0], excites, trans_table.shape[1]), F32),
        pltpu.VMEM(trans_table.shape[::-1], F32),
        pltpu.VMEM(row_map.shape, jnp.int32),
        pltpu.VMEM(coupling.shape, F32),
        pltpu.VMEM(schur_blocks.shape, BF16),
        pltpu.VMEM(near_blocks.shape, BF16),
        pltpu.VMEM((doms * unit, amount), BF16),
        pltpu.VMEM((halves, all_rows, slots), BF16),
        pltpu.VMEM((doms * unit, LANES), BF16),
        pltpu.VMEM((all_rows, LANES), BF16),
        pltpu.VMEM((2, subs, excites, rows), BF16),
        pltpu.VMEM((3 * subs, excites, rows), F32),
        pltpu.VMEM((boxes, excites, slots), F32),
        pltpu.VMEM((boxes * excites, directions), BF16),
        pltpu.VMEM((2, boxes * excites, directions), BF16),
        pltpu.VMEM((doms * boxes, excites, directions), F32),
        pltpu.VMEM((subs, excites, rows), F32),
        pltpu.VMEM((boxes, excites, slots), F32),
        pltpu.VMEM((boxes * excites, slots), BF16),
        pltpu.VMEM((all_rows, LANES), BF16),
        pltpu.VMEM((all_rows, LANES), BF16),
        dma((9,)),
        dma((subs,)),
        dma((2,)),
        dma((2,)),
        dma((2,)),
        dma((2,)),
        dma((2, 4)),
        dma((2, 4)),
    ]
    return pl.pallas_call(
        functools.partial(kernel, mesh_dims),
        out_shape=pltpu.VMEM(unknowns.shape, F32),
        in_specs=[hbm] * 4 + [vmem] * 2 + [hbm] * 6,
        out_specs=vmem,
        scratch_shapes=scratch,
        compiler_params=pltpu.CompilerParams(
            collective_id=0, has_side_effects=True, vmem_limit_bytes=56 * 1024 * 1024
        ),
    )(
        adjacency,
        inter_list.T,
        inter_type.T,
        near_list.T,
        unknowns,
        owner_box.reshape(1, amount),
        jnp.swapaxes(aggregation, 1, 2),
        trans_table.T,
        row_map,
        coupling,
        schur_blocks,
        near_blocks,
    )


def solution(mesh):
    in_specs = (
        P(("dom", "dir"), None, None),
        P(("dom", "dir"), None, None),
        P(("dom", "dir"), None),
        P(("dom", "dir"), None, None),
        P(("dom", "dir"), None, None),
        P(("dom", "dir"), None, None),
        P("dom", None, "dir"),
        P(None, "dir"),
        P("dom", None),
        P("dom", None),
        P(("dom", "dir"), None),
        P(("dom", "dir"), None, None, None),
    )
    out_specs = P(("dom", "dir"), None, None)
    dims = (mesh.shape["dom"], mesh.shape["dir"])
    return jax.shard_map(
        functools.partial(shards, dims),
        mesh=mesh,
        in_specs=in_specs,
        out_specs=out_specs,
        check_vma=False,
    )
```

```python
import functools

import jax
import jax.numpy as jnp
from jax import lax
from jax.experimental import pallas as pl
from jax.experimental.pallas import tpu as pltpu
from jax.sharding import PartitionSpec as P

MESH = pl.DeviceIdType.MESH
LANES = 128
F32 = jnp.float32
BF16 = jnp.bfloat16


def dot(a, b, ca, cb):
    return lax.dot_general(a, b, (((ca,), (cb,)), ((), ())), preferred_element_type=F32)


def iota(shape, dim):
    return lax.broadcasted_iota(jnp.int32, shape, dim)


def shift_of(value):
    bits = value.bit_length() - 1
    assert value == 1 << bits
    return bits


def kernel(
    dims,
    adj_hbm,
    list_hbm,
    type_hbm,
    near_hbm,
    unk_ref,
    owner_ref,
    agg_hbm,
    trans_hbm,
    maps_hbm,
    coup_hbm,
    schur_hbm,
    blocks_hbm,
    out_ref,
    adj_ref,
    list_ref,
    type_ref,
    near_ref,
    agg_v,
    trans_v,
    trans_t,
    maps_v,
    coup_v,
    schur_v,
    blocks_v,
    place,
    perm,
    send1,
    recv1,
    recv0,
    winf,
    curf,
    pats,
    recv2,
    patf,
    coupled,
    nearf,
    total,
    send3,
    recv3,
    local_sem,
    schur_sem,
    send_sem,
    recv_sem,
    side_send,
    side_recv,
    wide_send,
    wide_recv,
):
    doms, dirs = dims
    devices = doms * dirs
    subs, excites, rows = unk_ref.shape
    boxes, directions, slots = agg_v.shape
    near_count, own = near_ref.shape
    adj_count = adj_ref.shape[1]
    list_len = list_ref.shape[0]
    surface = owner_ref.shape[1] // subs
    capacity = slots // devices
    per_tile = LANES // excites
    halves = boxes // per_tile
    unit = max(16, halves * capacity)
    amount = subs * surface
    all_rows = devices * unit
    my_dom = lax.axis_index("dom")
    my_dir = lax.axis_index("dir")
    me = my_dom * dirs + my_dir
    my_slot = my_dir * doms + my_dom
    right, left = lax.rem(my_dom + 1, doms), lax.rem(my_dom + doms - 1, doms)
    odd = lax.rem(my_dom, 2)
    partner = my_dom + 1 - 2 * odd
    relay_to = lax.rem(my_dom + 2 - 4 * odd + doms, doms)
    relay_from = lax.rem(my_dom - 2 + 4 * odd + doms, doms)
    relay_source = relay_from + 1 - 2 * odd

    barrier = pltpu.get_barrier_semaphore()

    def greet(k, carry):
        other = lax.rem(me + k, devices)
        pl.semaphore_signal(
            barrier,
            inc=1,
            device_id=(lax.div(other, dirs), lax.rem(other, dirs)),
            device_id_type=MESH,
        )
        return carry

    lax.fori_loop(1, devices, greet, 0)

    locals_ = [
        pltpu.make_async_copy(src, dst, local_sem.at[i])
        for i, (src, dst) in enumerate(
            [
                (agg_hbm, agg_v),
                (trans_hbm, trans_t),
                (maps_hbm, maps_v),
                (coup_hbm, coup_v),
                (blocks_hbm, blocks_v),
                (adj_hbm, adj_ref),
                (list_hbm, list_ref),
                (type_hbm, type_ref),
                (near_hbm, near_ref),
            ]
        )
    ]
    schurs = [
        pltpu.make_async_copy(schur_hbm.at[s], schur_v.at[s], schur_sem.at[s]) for s in range(subs)
    ]
    locals_[0].start()
    schurs[0].start()
    schurs[1].start()
    locals_[4].start()
    for i in (1, 2, 3, 5, 6, 7, 8):
        locals_[i].start()
    for s in range(2, subs):
        schurs[s].start()

    owner_row = owner_ref[...]
    owner_col = jnp.concatenate(
        [
            jnp.broadcast_to(owner_row[:, k : k + LANES], (LANES, LANES)).T
            for k in range(0, amount, LANES)
        ],
        axis=0,
    )
    ahead = iota((LANES, LANES), 0) < iota((LANES, LANES), 1)
    ranks = []
    for k in range(0, amount, LANES):
        piece = owner_row[:, k : k + LANES]
        same = (owner_col[k : k + LANES] == piece) & ahead
        count = jnp.sum(jnp.where(same, 1.0, 0.0), axis=0, keepdims=True)
        if k > 0:
            earlier = jnp.where(owner_col[:k] == piece, 1.0, 0.0)
            count = count + jnp.sum(earlier, axis=0, keepdims=True)
        ranks.append(count)
    rank = jnp.concatenate(ranks, axis=1).astype(jnp.int32)
    half = (owner_row & (boxes - 1)) >> shift_of(per_tile)
    key = (owner_row >> shift_of(boxes)) * unit + half * capacity + rank
    place[...] = jnp.where(iota((doms * unit, amount), 0) == key, 1.0, 0.0).astype(BF16)
    wide = []
    for s in range(subs):
        piece = unk_ref[s][:, :surface].astype(F32)
        wide.append(jnp.concatenate([piece] * per_tile, axis=0).T)
    wide = jnp.concatenate(wide, axis=0)
    lane_box = iota((amount, LANES), 1) >> shift_of(excites)
    wide = jnp.where((owner_col & (per_tile - 1)) == lane_box, wide, 0.0).astype(BF16)
    send1[...] = dot(place[...], wide, 1, 0).astype(BF16)

    pl.semaphore_wait(barrier, devices - 1)

    def tile(index):
        return pl.ds(pl.multiple_of(index * unit, unit), unit)

    def scatter(k, carry):
        other = lax.rem(me + k, devices)
        to_dom, to_dir = lax.div(other, dirs), lax.rem(other, dirs)
        pltpu.make_async_remote_copy(
            src_ref=send1.at[tile(to_dom)],
            dst_ref=recv1.at[tile(my_slot)],
            send_sem=send_sem.at[0],
            recv_sem=recv_sem.at[0],
            device_id=(to_dom, to_dir),
            device_id_type=MESH,
        ).start()
        return carry

    lax.fori_loop(1, devices, scatter, 0)
    recv1[tile(my_slot), :] = send1[tile(my_dom), :]

    sides = []
    for side, target in enumerate((right, left)):
        copy = pltpu.make_async_remote_copy(
            src_ref=unk_ref,
            dst_ref=recv0.at[side],
            send_sem=side_send.at[side],
            recv_sem=side_recv.at[side],
            device_id=(target, my_dir),
            device_id_type=MESH,
        )
        copy.start()
        sides.append(copy)

    row = iota((all_rows, slots), 0)
    col = iota((all_rows, slots), 1)
    within = row & (unit - 1)
    slot_of = (row >> shift_of(unit)) * capacity + (within & (capacity - 1))
    for h in range(halves):
        hit = (slot_of == col) & ((within >> shift_of(capacity)) == h)
        perm[h] = jnp.where(hit, 1.0, 0.0).astype(BF16)

    def schur(s):
        schurs[s].wait()
        unknown = unk_ref[s]
        out_ref[s] = dot(unknown, schur_v[s], 1, 1)

    schur(0)
    schur(1)

    def drain(buffer, sem):
        size = pl.ds(0, all_rows - unit)
        pltpu.make_async_copy(buffer.at[size], buffer.at[size], sem).wait()

    drain(recv1, recv_sem.at[0])
    arrived = recv1[...]
    for h in range(halves):
        piece = dot(arrived, perm[h], 0, 0)
        curf[h * per_tile : (h + 1) * per_tile] = piece.reshape(per_tile, excites, slots)

    locals_[0].wait()
    chunks = 4
    chunk_boxes = boxes // chunks
    pair = 8
    wides = []
    for c in range(chunks):

        def radiate(i, carry):
            first = c * chunk_boxes + i * pair
            found = []
            for k in range(pair):
                b = first + k
                found.append(dot(curf[b].astype(BF16), agg_v[b], 1, 1))
            both = jnp.concatenate(found, axis=0).astype(BF16)
            size = pair * excites
            pats[pl.ds(pl.multiple_of(first * excites, size), size), :] = both
            patf[pl.ds(my_dom * boxes + first, pair)] = both.astype(F32).reshape(pair, excites, directions)
            return carry

        lax.fori_loop(0, chunk_boxes // pair, radiate, 0)
        at = pl.ds(c * chunk_boxes * excites, chunk_boxes * excites)
        copy = pltpu.make_async_remote_copy(
            src_ref=pats.at[at],
            dst_ref=recv2.at[0, at],
            send_sem=wide_send.at[0, c],
            recv_sem=wide_recv.at[0, c],
            device_id=(partner, my_dir),
            device_id_type=MESH,
        )
        copy.start()
        wides.append(copy)

    relays = []

    def relay(c):
        wides[c].wait_recv()
        at = pl.ds(c * chunk_boxes * excites, chunk_boxes * excites)
        copy = pltpu.make_async_remote_copy(
            src_ref=recv2.at[0, at],
            dst_ref=recv2.at[1, at],
            send_sem=wide_send.at[1, c],
            recv_sem=wide_recv.at[1, c],
            device_id=(relay_to, my_dir),
            device_id_type=MESH,
        )
        copy.start()
        relays.append(copy)

    for i in (2, 3, 5, 6, 7, 8):
        locals_[i].wait()

    locals_[4].wait()
    nearf[...] = jnp.zeros_like(nearf)

    def near(b):
        field = jnp.zeros((excites, slots), F32)
        for j in range(near_count):
            source = curf[near_ref[j, b]].astype(BF16)
            field = field + dot(source, blocks_v[b, j], 1, 1)
        nearf[my_dir * own + b] = field

    relay(0)
    locals_[1].wait()
    turned = trans_t[...].T
    trans_v[...] = jnp.broadcast_to(
        turned[:, None, :], (turned.shape[0], excites, turned.shape[1])
    )
    for b in range(own):
        near(b)
        if b + 1 in (own // 2, own * 3 // 4, own):
            relay((own // 2, own * 3 // 4, own).index(b + 1) + 1)
    for copy in sides:
        copy.wait_recv()
    winf[0:subs] = recv0[0].astype(F32)
    winf[subs : 2 * subs] = unk_ref[...].astype(F32)
    winf[2 * subs : 3 * subs] = recv0[1].astype(F32)
    group_subs = subs * dirs
    sub_base = left * group_subs

    def couple(s, carry):
        fields = [jnp.zeros((excites, LANES), F32)] * (rows // LANES)
        for k in range(adj_count):
            offset = adj_ref[s, k] - sub_base
            offset = jnp.where(offset < 0, offset + group_subs * doms, offset)
            offset = jnp.minimum(offset, 3 * group_subs - 1)
            source = winf[lax.div(offset, group_subs) * subs + lax.rem(offset, subs)]
            mapping = maps_v[s, k : k + 1, :]
            factor = coup_v[s, k : k + 1, :]
            for c in range(rows // LANES):
                at = slice(c * LANES, (c + 1) * LANES)
                index = jnp.broadcast_to(mapping[:, at], (excites, LANES))
                low, high = index & (LANES - 1), index >> shift_of(LANES)
                value = jnp.zeros((excites, LANES), F32)
                for q in range(rows // LANES):
                    got = jnp.take_along_axis(
                        source[:, q * LANES : (q + 1) * LANES],
                        low,
                        axis=1,
                        mode="promise_in_bounds",
                    )
                    value = jnp.where(high == q, got, value)
                fields[c] = fields[c] + factor[:, at] * value
        coupled[s] = jnp.concatenate(fields, axis=1)
        return carry

    lax.fori_loop(0, subs, couple, 0)

    for s in range(2, subs - 1):
        schur(s)

    for copy in relays:
        copy.wait_recv()
    for side, source in enumerate((partner, relay_source)):
        patf[pl.ds(source * boxes, boxes)] = recv2[side].astype(F32).reshape(boxes, excites, directions)

    def respond(i, carry):
        first = i * pair
        found = []
        for k in range(pair):
            b = first + k
            field = jnp.zeros((excites, directions), F32)
            for j in range(list_len):
                field = field + trans_v[type_ref[j, b]] * patf[list_ref[j, b]]
            found.append(dot(field.astype(BF16), agg_v[b], 1, 0) + nearf[b])
        both = jnp.concatenate(found, axis=0).astype(BF16)
        size = pair * excites
        total[pl.ds(pl.multiple_of(first * excites, size), size), :] = both
        return carry

    lax.fori_loop(0, boxes // pair, respond, 0)
    leaving = jnp.zeros((all_rows, LANES), F32)
    for h in range(halves):
        leaving = leaving + dot(perm[h], total[h * LANES : (h + 1) * LANES, :], 1, 1)
    send3[...] = leaving.astype(BF16)

    def give_back(k, carry):
        other = lax.rem(me + k, devices)
        to_dom, to_dir = lax.div(other, dirs), lax.rem(other, dirs)
        pltpu.make_async_remote_copy(
            src_ref=send3.at[tile(to_dir * doms + to_dom)],
            dst_ref=recv3.at[tile(my_slot)],
            send_sem=send_sem.at[1],
            recv_sem=recv_sem.at[1],
            device_id=(to_dom, to_dir),
            device_id_type=MESH,
        ).start()
        return carry

    lax.fori_loop(1, devices, give_back, 0)
    recv3[tile(my_slot), :] = send3[tile(my_slot), :]

    schur(subs - 1)

    drain(recv3, recv_sem.at[1])
    group_rows = doms * unit
    field = jnp.zeros((group_rows, LANES), F32)
    for r in range(dirs):
        field = field + recv3[r * group_rows : (r + 1) * group_rows, :].astype(F32)
    back = dot(field.T.astype(BF16), place[...], 1, 0)
    sub_box = iota((LANES, amount), 0) >> shift_of(excites)
    back = jnp.where((owner_row & (per_tile - 1)) == sub_box, back, 0.0)
    back = jnp.sum(back.reshape(per_tile, excites, amount), axis=0)
    for s in range(subs):
        add = coupled[s]
        out_ref[s, :, :surface] += add[:, :surface] + back[:, s * surface : (s + 1) * surface]
        out_ref[s, :, surface:] += add[:, surface:]

    for copy in sides:
        copy.wait_send()
    for copy in wides + relays:
        copy.wait_send()
    drain(recv1, send_sem.at[0])
    drain(recv3, send_sem.at[1])


def shards(
    mesh_dims,
    unknowns,
    schur_blocks,
    adjacency,
    row_map,
    coupling,
    owner_box,
    aggregation,
    trans_table,
    inter_list,
    inter_type,
    near_list,
    near_blocks,
):
    doms, dirs = mesh_dims
    subs, excites, rows = unknowns.shape
    boxes, slots, directions = aggregation.shape
    capacity = slots // (doms * dirs)
    per_tile = LANES // excites
    halves = boxes // per_tile
    unit = max(16, halves * capacity)
    all_rows = doms * dirs * unit
    amount = subs * owner_box.shape[1]
    vmem = pl.BlockSpec(memory_space=pltpu.VMEM)
    hbm = pl.BlockSpec(memory_space=pl.ANY)
    dma = pltpu.SemaphoreType.DMA
    smem = [
        pltpu.SMEM(value.shape, jnp.int32)
        for value in (adjacency, inter_list.T, inter_type.T, near_list.T)
    ]
    scratch = smem + [
        pltpu.VMEM((boxes, directions, slots), BF16),
        pltpu.VMEM((trans_table.shape[0], excites, trans_table.shape[1]), F32),
        pltpu.VMEM(trans_table.shape[::-1], F32),
        pltpu.VMEM(row_map.shape, jnp.int32),
        pltpu.VMEM(coupling.shape, F32),
        pltpu.VMEM(schur_blocks.shape, BF16),
        pltpu.VMEM(near_blocks.shape, BF16),
        pltpu.VMEM((doms * unit, amount), BF16),
        pltpu.VMEM((halves, all_rows, slots), BF16),
        pltpu.VMEM((doms * unit, LANES), BF16),
        pltpu.VMEM((all_rows, LANES), BF16),
        pltpu.VMEM((2, subs, excites, rows), BF16),
        pltpu.VMEM((3 * subs, excites, rows), F32),
        pltpu.VMEM((boxes, excites, slots), F32),
        pltpu.VMEM((boxes * excites, directions), BF16),
        pltpu.VMEM((2, boxes * excites, directions), BF16),
        pltpu.VMEM((doms * boxes, excites, directions), F32),
        pltpu.VMEM((subs, excites, rows), F32),
        pltpu.VMEM((boxes, excites, slots), F32),
        pltpu.VMEM((boxes * excites, slots), BF16),
        pltpu.VMEM((all_rows, LANES), BF16),
        pltpu.VMEM((all_rows, LANES), BF16),
        dma((9,)),
        dma((subs,)),
        dma((2,)),
        dma((2,)),
        dma((2,)),
        dma((2,)),
        dma((2, 4)),
        dma((2, 4)),
    ]
    return pl.pallas_call(
        functools.partial(kernel, mesh_dims),
        out_shape=pltpu.VMEM(unknowns.shape, F32),
        in_specs=[hbm] * 4 + [vmem] * 2 + [hbm] * 6,
        out_specs=vmem,
        scratch_shapes=scratch,
        compiler_params=pltpu.CompilerParams(
            collective_id=0, has_side_effects=True, vmem_limit_bytes=56 * 1024 * 1024
        ),
    )(
        adjacency,
        inter_list.T,
        inter_type.T,
        near_list.T,
        unknowns,
        owner_box.reshape(1, amount),
        jnp.swapaxes(aggregation, 1, 2),
        trans_table.T,
        row_map,
        coupling,
        schur_blocks,
        near_blocks,
    )


def solution(mesh):
    in_specs = (
        P(("dom", "dir"), None, None),
        P(("dom", "dir"), None, None),
        P(("dom", "dir"), None),
        P(("dom", "dir"), None, None),
        P(("dom", "dir"), None, None),
        P(("dom", "dir"), None, None),
        P("dom", None, "dir"),
        P(None, "dir"),
        P("dom", None),
        P("dom", None),
        P(("dom", "dir"), None),
        P(("dom", "dir"), None, None, None),
    )
    out_specs = P(("dom", "dir"), None, None)
    dims = (mesh.shape["dom"], mesh.shape["dir"])
    return jax.shard_map(
        functools.partial(shards, dims),
        mesh=mesh,
        in_specs=in_specs,
        out_specs=out_specs,
        check_vma=False,
    )
```

```python
import functools

import jax
import jax.numpy as jnp
from jax import lax
from jax.experimental import pallas as pl
from jax.experimental.pallas import tpu as pltpu
from jax.sharding import PartitionSpec as P

MESH = pl.DeviceIdType.MESH
LANES = 128
F32 = jnp.float32
BF16 = jnp.bfloat16


def dot(a, b, ca, cb):
    return lax.dot_general(a, b, (((ca,), (cb,)), ((), ())), preferred_element_type=F32)


def iota(shape, dim):
    return lax.broadcasted_iota(jnp.int32, shape, dim)


def shift_of(value):
    bits = value.bit_length() - 1
    assert value == 1 << bits
    return bits


def kernel(
    dims,
    adj_hbm,
    list_hbm,
    type_hbm,
    near_hbm,
    unk_ref,
    owner_ref,
    agg_hbm,
    trans_hbm,
    maps_hbm,
    coup_hbm,
    schur_hbm,
    blocks_hbm,
    out_ref,
    adj_ref,
    list_ref,
    type_ref,
    near_ref,
    agg_v,
    trans_v,
    trans_t,
    maps_v,
    coup_v,
    schur_v,
    blocks_v,
    place,
    perm,
    send1,
    recv1,
    recv0,
    winf,
    curf,
    pats,
    recv2,
    patf,
    coupled,
    nearf,
    total,
    send3,
    recv3,
    local_sem,
    schur_sem,
    send_sem,
    recv_sem,
    side_send,
    side_recv,
    wide_send,
    wide_recv,
):
    doms, dirs = dims
    devices = doms * dirs
    subs, excites, rows = unk_ref.shape
    boxes, directions, slots = agg_v.shape
    near_count, own = near_ref.shape
    adj_count = adj_ref.shape[1]
    list_len = list_ref.shape[0]
    surface = owner_ref.shape[1] // subs
    capacity = slots // devices
    per_tile = LANES // excites
    halves = boxes // per_tile
    unit = max(16, halves * capacity)
    amount = subs * surface
    all_rows = devices * unit
    my_dom = lax.axis_index("dom")
    my_dir = lax.axis_index("dir")
    me = my_dom * dirs + my_dir
    my_slot = my_dir * doms + my_dom
    right, left = lax.rem(my_dom + 1, doms), lax.rem(my_dom + doms - 1, doms)
    odd = lax.rem(my_dom, 2)
    partner = my_dom + 1 - 2 * odd
    relay_to = lax.rem(my_dom + 2 - 4 * odd + doms, doms)
    relay_from = lax.rem(my_dom - 2 + 4 * odd + doms, doms)
    relay_source = relay_from + 1 - 2 * odd

    barrier = pltpu.get_barrier_semaphore()

    def greet(k, carry):
        other = lax.rem(me + k, devices)
        pl.semaphore_signal(
            barrier,
            inc=1,
            device_id=(lax.div(other, dirs), lax.rem(other, dirs)),
            device_id_type=MESH,
        )
        return carry

    lax.fori_loop(1, devices, greet, 0)

    locals_ = [
        pltpu.make_async_copy(src, dst, local_sem.at[i])
        for i, (src, dst) in enumerate(
            [
                (agg_hbm, agg_v),
                (trans_hbm, trans_t),
                (maps_hbm, maps_v),
                (coup_hbm, coup_v),
                (blocks_hbm, blocks_v),
                (adj_hbm, adj_ref),
                (list_hbm, list_ref),
                (type_hbm, type_ref),
                (near_hbm, near_ref),
            ]
        )
    ]
    schurs = [
        pltpu.make_async_copy(schur_hbm.at[s], schur_v.at[s], schur_sem.at[s]) for s in range(subs)
    ]
    locals_[0].start()
    schurs[0].start()
    schurs[1].start()
    locals_[4].start()
    for i in (1, 2, 3, 5, 6, 7, 8):
        locals_[i].start()
    for s in range(2, subs):
        schurs[s].start()

    owner_row = owner_ref[...]
    owner_col = jnp.concatenate(
        [
            jnp.broadcast_to(owner_row[:, k : k + LANES], (LANES, LANES)).T
            for k in range(0, amount, LANES)
        ],
        axis=0,
    )
    ahead = iota((LANES, LANES), 0) < iota((LANES, LANES), 1)
    ranks = []
    for k in range(0, amount, LANES):
        piece = owner_row[:, k : k + LANES]
        same = (owner_col[k : k + LANES] == piece) & ahead
        count = jnp.sum(jnp.where(same, 1.0, 0.0), axis=0, keepdims=True)
        if k > 0:
            earlier = jnp.where(owner_col[:k] == piece, 1.0, 0.0)
            count = count + jnp.sum(earlier, axis=0, keepdims=True)
        ranks.append(count)
    rank = jnp.concatenate(ranks, axis=1).astype(jnp.int32)
    half = (owner_row & (boxes - 1)) >> shift_of(per_tile)
    key = (owner_row >> shift_of(boxes)) * unit + half * capacity + rank
    place[...] = jnp.where(iota((doms * unit, amount), 0) == key, 1.0, 0.0).astype(BF16)
    wide = []
    for s in range(subs):
        piece = unk_ref[s][:, :surface].astype(F32)
        wide.append(jnp.concatenate([piece] * per_tile, axis=0).T)
    wide = jnp.concatenate(wide, axis=0)
    lane_box = iota((amount, LANES), 1) >> shift_of(excites)
    wide = jnp.where((owner_col & (per_tile - 1)) == lane_box, wide, 0.0).astype(BF16)
    send1[...] = dot(place[...], wide, 1, 0).astype(BF16)

    pl.semaphore_wait(barrier, devices - 1)

    def tile(index):
        return pl.ds(pl.multiple_of(index * unit, unit), unit)

    def scatter(k, carry):
        other = lax.rem(me + k, devices)
        to_dom, to_dir = lax.div(other, dirs), lax.rem(other, dirs)
        pltpu.make_async_remote_copy(
            src_ref=send1.at[tile(to_dom)],
            dst_ref=recv1.at[tile(my_slot)],
            send_sem=send_sem.at[0],
            recv_sem=recv_sem.at[0],
            device_id=(to_dom, to_dir),
            device_id_type=MESH,
        ).start()
        return carry

    lax.fori_loop(1, devices, scatter, 0)
    recv1[tile(my_slot), :] = send1[tile(my_dom), :]

    sides = []
    for side, target in enumerate((right, left)):
        copy = pltpu.make_async_remote_copy(
            src_ref=unk_ref,
            dst_ref=recv0.at[side],
            send_sem=side_send.at[side],
            recv_sem=side_recv.at[side],
            device_id=(target, my_dir),
            device_id_type=MESH,
        )
        copy.start()
        sides.append(copy)

    row = iota((all_rows, slots), 0)
    col = iota((all_rows, slots), 1)
    within = row & (unit - 1)
    slot_of = (row >> shift_of(unit)) * capacity + (within & (capacity - 1))
    for h in range(halves):
        hit = (slot_of == col) & ((within >> shift_of(capacity)) == h)
        perm[h] = jnp.where(hit, 1.0, 0.0).astype(BF16)

    def schur(s):
        schurs[s].wait()
        unknown = unk_ref[s]
        out_ref[s] = dot(unknown, schur_v[s], 1, 1)

    schur(0)
    schur(1)

    def drain(buffer, sem):
        size = pl.ds(0, all_rows - unit)
        pltpu.make_async_copy(buffer.at[size], buffer.at[size], sem).wait()

    drain(recv1, recv_sem.at[0])
    arrived = recv1[...]
    for h in range(halves):
        piece = dot(arrived, perm[h], 0, 0)
        curf[h * per_tile : (h + 1) * per_tile] = piece.reshape(per_tile, excites, slots)

    locals_[0].wait()
    chunks = 4
    chunk_boxes = boxes // chunks
    pair = 8
    wides = []
    for c in range(chunks):

        def radiate(i, carry):
            first = c * chunk_boxes + i * pair
            found = []
            for k in range(pair):
                b = first + k
                found.append(dot(curf[b].astype(BF16), agg_v[b], 1, 1))
            both = jnp.concatenate(found, axis=0).astype(BF16)
            size = pair * excites
            pats[pl.ds(pl.multiple_of(first * excites, size), size), :] = both
            patf[pl.ds(my_dom * boxes + first, pair)] = both.astype(F32).reshape(pair, excites, directions)
            return carry

        lax.fori_loop(0, chunk_boxes // pair, radiate, 0)
        at = pl.ds(c * chunk_boxes * excites, chunk_boxes * excites)
        copy = pltpu.make_async_remote_copy(
            src_ref=pats.at[at],
            dst_ref=recv2.at[0, at],
            send_sem=wide_send.at[0, c],
            recv_sem=wide_recv.at[0, c],
            device_id=(partner, my_dir),
            device_id_type=MESH,
        )
        copy.start()
        wides.append(copy)

    relays = []

    def relay(c):
        wides[c].wait_recv()
        at = pl.ds(c * chunk_boxes * excites, chunk_boxes * excites)
        copy = pltpu.make_async_remote_copy(
            src_ref=recv2.at[0, at],
            dst_ref=recv2.at[1, at],
            send_sem=wide_send.at[1, c],
            recv_sem=wide_recv.at[1, c],
            device_id=(relay_to, my_dir),
            device_id_type=MESH,
        )
        copy.start()
        relays.append(copy)

    for i in (2, 3, 5, 6, 7, 8):
        locals_[i].wait()

    locals_[4].wait()
    nearf[...] = jnp.zeros_like(nearf)

    def near(b):
        field = jnp.zeros((excites, slots), F32)
        for j in range(near_count):
            source = curf[near_ref[j, b]].astype(BF16)
            field = field + dot(source, blocks_v[b, j], 1, 1)
        nearf[my_dir * own + b] = field

    relay(0)
    locals_[1].wait()
    turned = trans_t[...].T
    trans_v[...] = jnp.broadcast_to(
        turned[:, None, :], (turned.shape[0], excites, turned.shape[1])
    )
    for b in range(own):
        near(b)
        if b + 1 in (own // 2, own * 3 // 4, own):
            relay((own // 2, own * 3 // 4, own).index(b + 1) + 1)
    for copy in sides:
        copy.wait_recv()
    winf[0:subs] = recv0[0].astype(F32)
    winf[subs : 2 * subs] = unk_ref[...].astype(F32)
    winf[2 * subs : 3 * subs] = recv0[1].astype(F32)
    group_subs = subs * dirs
    sub_base = left * group_subs

    def couple(s, carry):
        fields = [jnp.zeros((excites, LANES), F32)] * (rows // LANES)
        for k in range(adj_count):
            offset = adj_ref[s, k] - sub_base
            offset = jnp.where(offset < 0, offset + group_subs * doms, offset)
            offset = jnp.minimum(offset, 3 * group_subs - 1)
            source = winf[lax.div(offset, group_subs) * subs + lax.rem(offset, subs)]
            mapping = maps_v[s, k : k + 1, :]
            factor = coup_v[s, k : k + 1, :]
            for c in range(rows // LANES):
                at = slice(c * LANES, (c + 1) * LANES)
                index = jnp.broadcast_to(mapping[:, at], (excites, LANES))
                low, high = index & (LANES - 1), index >> shift_of(LANES)
                value = jnp.zeros((excites, LANES), F32)
                for q in range(rows // LANES):
                    got = jnp.take_along_axis(
                        source[:, q * LANES : (q + 1) * LANES],
                        low,
                        axis=1,
                        mode="promise_in_bounds",
                    )
                    value = jnp.where(high == q, got, value)
                fields[c] = fields[c] + factor[:, at] * value
        coupled[s] = jnp.concatenate(fields, axis=1)
        return carry

    lax.fori_loop(0, subs, couple, 0)

    for s in range(2, subs - 1):
        schur(s)

    for copy in relays:
        copy.wait_recv()
    for side, source in enumerate((partner, relay_source)):
        patf[pl.ds(source * boxes, boxes)] = recv2[side].astype(F32).reshape(boxes, excites, directions)

    batch = 16

    def respond(i, carry):
        first = i * batch
        found = []
        for k in range(batch):
            b = first + k
            field = jnp.zeros((excites, directions), F32)
            for j in range(list_len):
                field = field + trans_v[type_ref[j, b]] * patf[list_ref[j, b]]
            found.append(dot(field.astype(BF16), agg_v[b], 1, 0) + nearf[b])
        both = jnp.concatenate(found, axis=0).astype(BF16)
        size = batch * excites
        total[pl.ds(pl.multiple_of(first * excites, size), size), :] = both
        return carry

    lax.fori_loop(0, boxes // batch, respond, 0)
    leaving = jnp.zeros((all_rows, LANES), F32)
    for h in range(halves):
        leaving = leaving + dot(perm[h], total[h * LANES : (h + 1) * LANES, :], 1, 1)
    send3[...] = leaving.astype(BF16)

    def give_back(k, carry):
        other = lax.rem(me + k, devices)
        to_dom, to_dir = lax.div(other, dirs), lax.rem(other, dirs)
        pltpu.make_async_remote_copy(
            src_ref=send3.at[tile(to_dir * doms + to_dom)],
            dst_ref=recv3.at[tile(my_slot)],
            send_sem=send_sem.at[1],
            recv_sem=recv_sem.at[1],
            device_id=(to_dom, to_dir),
            device_id_type=MESH,
        ).start()
        return carry

    lax.fori_loop(1, devices, give_back, 0)
    recv3[tile(my_slot), :] = send3[tile(my_slot), :]

    schur(subs - 1)

    drain(recv3, recv_sem.at[1])
    group_rows = doms * unit
    field = jnp.zeros((group_rows, LANES), F32)
    for r in range(dirs):
        field = field + recv3[r * group_rows : (r + 1) * group_rows, :].astype(F32)
    back = dot(field.T.astype(BF16), place[...], 1, 0)
    sub_box = iota((LANES, amount), 0) >> shift_of(excites)
    back = jnp.where((owner_row & (per_tile - 1)) == sub_box, back, 0.0)
    back = jnp.sum(back.reshape(per_tile, excites, amount), axis=0)
    for s in range(subs):
        add = coupled[s]
        out_ref[s, :, :surface] += add[:, :surface] + back[:, s * surface : (s + 1) * surface]
        out_ref[s, :, surface:] += add[:, surface:]

    for copy in sides:
        copy.wait_send()
    for copy in wides + relays:
        copy.wait_send()
    drain(recv1, send_sem.at[0])
    drain(recv3, send_sem.at[1])


def shards(
    mesh_dims,
    unknowns,
    schur_blocks,
    adjacency,
    row_map,
    coupling,
    owner_box,
    aggregation,
    trans_table,
    inter_list,
    inter_type,
    near_list,
    near_blocks,
):
    doms, dirs = mesh_dims
    subs, excites, rows = unknowns.shape
    boxes, slots, directions = aggregation.shape
    capacity = slots // (doms * dirs)
    per_tile = LANES // excites
    halves = boxes // per_tile
    unit = max(16, halves * capacity)
    all_rows = doms * dirs * unit
    amount = subs * owner_box.shape[1]
    vmem = pl.BlockSpec(memory_space=pltpu.VMEM)
    hbm = pl.BlockSpec(memory_space=pl.ANY)
    dma = pltpu.SemaphoreType.DMA
    smem = [
        pltpu.SMEM(value.shape, jnp.int32)
        for value in (adjacency, inter_list.T, inter_type.T, near_list.T)
    ]
    scratch = smem + [
        pltpu.VMEM((boxes, directions, slots), BF16),
        pltpu.VMEM((trans_table.shape[0], excites, trans_table.shape[1]), F32),
        pltpu.VMEM(trans_table.shape[::-1], F32),
        pltpu.VMEM(row_map.shape, jnp.int32),
        pltpu.VMEM(coupling.shape, F32),
        pltpu.VMEM(schur_blocks.shape, BF16),
        pltpu.VMEM(near_blocks.shape, BF16),
        pltpu.VMEM((doms * unit, amount), BF16),
        pltpu.VMEM((halves, all_rows, slots), BF16),
        pltpu.VMEM((doms * unit, LANES), BF16),
        pltpu.VMEM((all_rows, LANES), BF16),
        pltpu.VMEM((2, subs, excites, rows), BF16),
        pltpu.VMEM((3 * subs, excites, rows), F32),
        pltpu.VMEM((boxes, excites, slots), F32),
        pltpu.VMEM((boxes * excites, directions), BF16),
        pltpu.VMEM((2, boxes * excites, directions), BF16),
        pltpu.VMEM((doms * boxes, excites, directions), F32),
        pltpu.VMEM((subs, excites, rows), F32),
        pltpu.VMEM((boxes, excites, slots), F32),
        pltpu.VMEM((boxes * excites, slots), BF16),
        pltpu.VMEM((all_rows, LANES), BF16),
        pltpu.VMEM((all_rows, LANES), BF16),
        dma((9,)),
        dma((subs,)),
        dma((2,)),
        dma((2,)),
        dma((2,)),
        dma((2,)),
        dma((2, 4)),
        dma((2, 4)),
    ]
    return pl.pallas_call(
        functools.partial(kernel, mesh_dims),
        out_shape=pltpu.VMEM(unknowns.shape, F32),
        in_specs=[hbm] * 4 + [vmem] * 2 + [hbm] * 6,
        out_specs=vmem,
        scratch_shapes=scratch,
        compiler_params=pltpu.CompilerParams(
            collective_id=0, has_side_effects=True, vmem_limit_bytes=56 * 1024 * 1024
        ),
    )(
        adjacency,
        inter_list.T,
        inter_type.T,
        near_list.T,
        unknowns,
        owner_box.reshape(1, amount),
        jnp.swapaxes(aggregation, 1, 2),
        trans_table.T,
        row_map,
        coupling,
        schur_blocks,
        near_blocks,
    )


def solution(mesh):
    in_specs = (
        P(("dom", "dir"), None, None),
        P(("dom", "dir"), None, None),
        P(("dom", "dir"), None),
        P(("dom", "dir"), None, None),
        P(("dom", "dir"), None, None),
        P(("dom", "dir"), None, None),
        P("dom", None, "dir"),
        P(None, "dir"),
        P("dom", None),
        P("dom", None),
        P(("dom", "dir"), None),
        P(("dom", "dir"), None, None, None),
    )
    out_specs = P(("dom", "dir"), None, None)
    dims = (mesh.shape["dom"], mesh.shape["dir"])
    return jax.shard_map(
        functools.partial(shards, dims),
        mesh=mesh,
        in_specs=in_specs,
        out_specs=out_specs,
        check_vma=False,
    )
```
